512 devices in a mesh: ep: 64 (over z, x, core), dp: 8 (over y).
Axes of the slice: x: 4, y: 8, z: 8, core: 2. Of those that a mesh axis runs over, the one named last changes fastest.
Arguments:
- tokens: bfloat16 [4096, 4096], P('ep', 'dp'), may hold values from -6 to 6
- expert_ids: int32 [4096, 8], P('ep'), may hold values from 0 to 63, all different within a row
- gate_logits: float32 [4096, 8], P('ep'), may hold values from -6 to 6
- placement: int32 [32], replicated, may hold values from 0 to 63, as said below
- split_rows: int32 [32], replicated, may hold values from 0 to 8
- gate_up_weight: bfloat16 [64, 4096, 2, 1024], P('ep', None, None, 'dp'), may hold values from -0.09375 to 0.09375
- down_weight: bfloat16 [64, 1024, 4096], P('ep', None, 'dp'), may hold values from -0.1875 to 0.1875
- spare_gate_up: bfloat16 [64, 4096, 2, 512], P('ep', None, None, 'dp'), may hold values from -0.09375 to 0.09375
- spare_down: bfloat16 [64, 512, 4096], P('ep', None, 'dp'), may hold values from -0.1875 to 0.1875
Outputs:
- mixed: bfloat16 [4096, 4096], P('ep', 'dp')
The draws below stay inside these ranges and needn't reach their ends.
Inputs may be any that keep to these rules, and one draw needn't show every extreme that they name: `expert_ids`: each token names 8 different experts. `placement`: 32 different experts.
All inputs are finite; a program needn't handle non-finite values.
Results may differ from the reference program's by a relative error of at most 0.0058.
Values may be sent and summed in bfloat16 or wider, within the bound.
A program may use at most 64 MiB of HBM per device.

```python
import jax
import jax.numpy as jnp
from jax import lax

D = 4096
FF = 1024
TOPK = 8
TOK_GRP = 64
EXPERTS = 64
REDUNDANT = 32
TOKENS = 4096
CAP = 8


def draw_placement(key, part):
    return jax.random.permutation(key, EXPERTS)[:REDUNDANT].astype(jnp.int32)


def draw_split_rows(key, part):
    first_key = jax.random.fold_in(key, 11)
    second_key = jax.random.fold_in(key, 23)
    values = jax.random.randint(first_key, (REDUNDANT,), 0, CAP + 1)
    spot = jax.random.randint(second_key, (), 0, REDUNDANT)
    order = jnp.arange(REDUNDANT)
    values = jnp.where(order == spot, CAP, values)
    values = jnp.where(order == (spot + 1) % REDUNDANT, 0, values)
    return values.astype(jnp.int32)


def shard_levels(own_key, extent, shards, low, largest):
    def one(dim, blocks):
        steps = jax.random.uniform(jax.random.fold_in(jax.random.fold_in(own_key, 6), dim), (blocks,), jnp.float32, low / len(shards), largest / len(shards))
        return jnp.repeat(jnp.exp(steps), extent[dim] // blocks).reshape((-1,) + (1,) * (len(extent) - dim - 1))

    loudness = one(*shards[0])
    for cut in shards[1:]:
        loudness = loudness * one(*cut)
    return loudness


def different_ones(stream_key, rows, amount, top, lift):
    ranking = jax.random.permutation(jax.random.fold_in(stream_key, 1), amount)
    boost = ranking
    for power in range(3):
        boost = boost * boost // amount
    boost = boost * lift // amount
    chance = jax.random.randint(jax.random.fold_in(stream_key, 2), (rows, amount), 0, 4096) + boost
    sure = jax.random.permutation(jax.random.fold_in(stream_key, 3), rows)[jnp.arange(amount) % rows]
    chance = jnp.where(jnp.arange(rows)[:, None] == sure[None, :], 1 << 14, chance)
    merit = chance * amount + jnp.arange(amount)
    return lax.top_k(merit.astype(jnp.int32), top)[1].astype(jnp.int32)


def scatter_about(key, extent, spread, bound, pieces=(), kind=jnp.bfloat16):
    result = spread * jax.random.normal(key, extent, jnp.float32)
    if pieces:
        result = result * shard_levels(key, extent, pieces, -0.22, 0.18)
    return jnp.clip(result, -bound, bound).astype(kind)


def setup_inputs(seed: int = 0) -> dict:
    splits = jax.random.split(jax.random.key(seed), 10)
    return {
        "tokens": scatter_about(splits[0], (TOKENS, D), 1.0, 6.0, ((0, 64), (1, 8))),
        "expert_ids": different_ones(splits[1], TOKENS, EXPERTS, TOPK, 1024),
        "gate_logits": scatter_about(splits[2], (TOKENS, TOPK), 1.5, 6.0, ((0, 64),), jnp.float32),
        "placement": draw_placement(jax.random.fold_in(splits[9], 71), 0),
        "split_rows": draw_split_rows(jax.random.fold_in(splits[9], 71), 0),
        "gate_up_weight": scatter_about(splits[5], (EXPERTS, D, 2, FF), D ** -0.5, 0.09375, ((0, 64), (3, 8))),
        "down_weight": scatter_about(splits[6], (EXPERTS, FF, D), FF ** -0.5, 0.1875, ((0, 64), (2, 8))),
        "spare_gate_up": scatter_about(splits[7], (2 * REDUNDANT, D, 2, FF // 2), D ** -0.5, 0.09375, ((0, 64), (3, 8))),
        "spare_down": scatter_about(splits[8], (2 * REDUNDANT, FF // 2, D), FF ** -0.5, 0.1875, ((0, 64), (2, 8))),
    }


def assign_slots(expert_ids, placement, split_rows):
    per_group = TOK_GRP * TOPK
    chosen_ids = expert_ids.reshape(-1, per_group)
    ordinal = jnp.arange(per_group, dtype=jnp.int32)
    earlier = ordinal[None, :] < ordinal[:, None]
    same_expert = chosen_ids[:, :, None] == chosen_ids[:, None, :]
    pair_rank = jnp.sum(jnp.where(same_expert & earlier[None], 1, 0), axis=2).astype(jnp.int32)
    is_match = chosen_ids[:, :, None] == placement[None, None, :]
    is_hot = jnp.any(is_match, axis=2)
    copy_index = jnp.sum(jnp.where(is_match, jnp.arange(REDUNDANT, dtype=jnp.int32)[None, None, :], 0), axis=2).astype(jnp.int32)
    split_here = jnp.sum(jnp.where(is_match, split_rows[None, None, :], 0), axis=2).astype(jnp.int32)
    to_copy = is_hot & (pair_rank >= split_here)
    slot_of = jnp.where(to_copy, EXPERTS + copy_index, chosen_ids).astype(jnp.int32)
    position = jnp.where(to_copy, pair_rank - split_here, pair_rank).astype(jnp.int32)
    kept_mask = position < CAP
    return slot_of, position, kept_mask


def run_slot(token_rows, both_weight, down_part):
    gate_both = jnp.dot(token_rows, both_weight.reshape(D, 2 * FF), preferred_element_type=jnp.float32)
    gate_both = gate_both.reshape(token_rows.shape[0], 2, FF)
    hidden = (jax.nn.silu(gate_both[:, 0, :]) * gate_both[:, 1, :]).astype(jnp.bfloat16)
    return jnp.dot(hidden, down_part, preferred_element_type=jnp.float32).astype(jnp.bfloat16)


def reference(tokens, expert_ids, gate_logits, placement, split_rows, gate_up_weight, down_weight, spare_gate_up, spare_down):
    gate_score = jax.nn.sigmoid(gate_logits.astype(jnp.float32))
    gate_weight = 2.5 * gate_score / jnp.sum(gate_score, axis=1, keepdims=True)
    slot_of, position, kept_mask = assign_slots(expert_ids, placement, split_rows)
    groups = TOKENS // TOK_GRP
    per_group = TOK_GRP * TOPK
    slot_count = EXPERTS + REDUNDANT
    slot_total = slot_count * groups * CAP
    group_of = jnp.arange(groups, dtype=jnp.int32)[:, None]
    flat_index = ((slot_of * groups + group_of) * CAP + position).astype(jnp.int32)
    owner_token = (group_of * TOK_GRP + jnp.arange(per_group, dtype=jnp.int32)[None, :] // TOPK).astype(jnp.int32)
    row_table = jnp.full((slot_total,), TOKENS, jnp.int32)
    row_table = row_table.at[jnp.where(kept_mask, flat_index, slot_total)].set(owner_token, mode="drop")
    row_table = row_table.reshape(slot_count, groups * CAP)
    padded = jnp.concatenate([tokens, jnp.zeros((1, D), tokens.dtype)], axis=0)
    spare_gu_all = spare_gate_up.reshape(REDUNDANT, 2, D, 2, FF // 2)
    spare_dn_all = spare_down.reshape(REDUNDANT, 2, FF // 2, D)

    def home_slot(slot_index):
        token_rows = jnp.take(padded, row_table[slot_index], axis=0)
        return run_slot(token_rows, gate_up_weight[slot_index], down_weight[slot_index])

    def spare_slot(spare_index):
        token_rows = jnp.take(padded, row_table[EXPERTS + spare_index], axis=0)
        both_weight = jnp.transpose(spare_gu_all[spare_index], (1, 2, 0, 3)).reshape(D, 2, FF)
        down_part = spare_dn_all[spare_index].reshape(FF, D)
        return run_slot(token_rows, both_weight, down_part)

    home_out = lax.map(home_slot, jnp.arange(EXPERTS, dtype=jnp.int32))
    spare_out = lax.map(spare_slot, jnp.arange(REDUNDANT, dtype=jnp.int32))
    flat_out = jnp.concatenate([home_out, spare_out], axis=0).reshape(slot_total, D)
    picked = jnp.take(flat_out, jnp.where(kept_mask, flat_index, 0), axis=0)
    kept_weight = jnp.where(kept_mask, gate_weight.reshape(groups, per_group), 0.0)
    mixed = jnp.sum((kept_weight[:, :, None] * picked.astype(jnp.float32)).reshape(TOKENS, TOPK, D), axis=1)
    return mixed.astype(jnp.bfloat16)
```

```python
import functools

import jax
import jax.numpy as jnp
from jax import lax
from jax.experimental import pallas as pl
from jax.experimental.pallas import tpu as pltpu
from jax.sharding import PartitionSpec as P

MESH = pl.DeviceIdType.MESH
F32 = jnp.float32
BF16 = jnp.bfloat16
CHUNKS = 4
CW, CCW = 0, 1


def hops(chunk, way):
    return 4 if chunk % 2 == way else 3


def expert_kernel(
    rows_ref, wh_ref, ws_ref, dh_ref, ds_ref, out_ref,
    feat, pair_feat, hid, acc_h, acc_s, dspare, part, pair_part,
    ring_send, ring_recv, pair_send, pair_recv, hid_send, hid_recv, part_send, part_recv,
):
    n_dp = 8
    ep = lax.axis_index("ep")
    me = lax.axis_index("dp")
    core = lax.rem(ep, 2)
    sibling = {"ep": ep + 1 - 2 * core, "dp": me}
    ring = (
        {"ep": ep, "dp": lax.rem(me + 1, n_dp)},
        {"ep": ep, "dp": lax.rem(me + n_dp - 1, n_dp)},
    )
    total = rows_ref.shape[0]
    rows = total // CHUNKS
    width = wh_ref.shape[0] // n_dp
    half = width // 2
    units = wh_ref.shape[1] // 2

    barrier = pltpu.get_barrier_semaphore()
    for other in (ring[0], ring[1], sibling):
        pl.semaphore_signal(barrier, inc=1, device_id=other, device_id_type=MESH)
    pl.semaphore_wait(barrier, 3)

    def source(way, hop):
        return lax.rem(me + (n_dp - hop if way == CW else hop), n_dp)

    def feat_copy(chunk, way, hop):
        src = source(way, hop - 1)
        window = pl.ds(chunk * rows, rows)
        return pltpu.make_async_remote_copy(
            src_ref=rows_ref.at[window] if hop == 1 else feat.at[src, window],
            dst_ref=feat.at[src, window],
            send_sem=ring_send.at[chunk, way, hop - 1],
            recv_sem=ring_recv.at[chunk, way, hop - 1],
            device_id=ring[way], device_id_type=MESH,
        )

    def pair_copy(chunk, way, hop):
        src = source(way, hop)
        window = pl.ds(chunk * rows, rows)
        block = rows_ref.at[window, pl.ds(width, half)] if hop == 0 else feat.at[src, window, pl.ds(width, half)]
        return pltpu.make_async_remote_copy(
            src_ref=block,
            dst_ref=pair_feat.at[src, window],
            send_sem=pair_send.at[chunk, way, hop],
            recv_sem=pair_recv.at[chunk, way, hop],
            device_id=sibling, device_id_type=MESH,
        )

    hid_rows = rows + rows // 2

    def hid_copy(chunk, way, hop):
        src = source(way, hop - 1)
        window = pl.ds(chunk * hid_rows, hid_rows)
        return pltpu.make_async_remote_copy(
            src_ref=hid.at[src, window],
            dst_ref=hid.at[src, window],
            send_sem=hid_send.at[chunk, way, hop - 1],
            recv_sem=hid_recv.at[chunk, way, hop - 1],
            device_id=ring[way], device_id_type=MESH,
        )

    out_half = ds_ref.shape[1] // 2

    def part_copy(chunk):
        window = pl.ds(chunk * rows, rows)
        return pltpu.make_async_remote_copy(
            src_ref=part.at[window, pl.ds((1 - core) * out_half, out_half)],
            dst_ref=pair_part.at[window],
            send_sem=part_send.at[chunk],
            recv_sem=part_recv.at[chunk],
            device_id=sibling, device_id_type=MESH,
        )

    def begin(chunk):
        for way in (CW, CCW):
            feat_copy(chunk, way, 1).start()
        pair_copy(chunk, CW, 0).start()

    def first_half(chunk):
        window = pl.ds(chunk * rows, rows)
        for way in (CW, CCW):
            for hop in range(0 if way == CW else 1, hops(chunk, way) + 1):
                pair_copy(chunk, way, hop).wait_recv()

        def term(block, other, at):
            x = block[:, :width]
            w = wh_ref[pl.ds(pl.multiple_of(at * width, width), width), :]
            home = jnp.dot(x, w, preferred_element_type=F32)
            own_at = pl.ds(pl.multiple_of(at * width + core * half, half), half)
            other_at = pl.ds(pl.multiple_of(at * width + (1 - core) * half, half), half)
            dims = (((1,), (1,)), ((), ()))
            spare = lax.dot_general(block[:, width:], ws_ref[:, own_at], dims, preferred_element_type=F32)
            spare += lax.dot_general(other, ws_ref[:, other_at], dims, preferred_element_type=F32)
            return home, spare

        acc_h[...], acc_s[...] = term(rows_ref[window, :], pair_feat[me, window, :], me)

        @pl.loop(1, n_dp)
        def _(step):
            at = lax.rem(me + step, n_dp)
            home, spare = term(feat[at, window, :], pair_feat[at, window, :], at)
            acc_h[...] += home
            acc_s[...] += spare

        gate = acc_h[:, :units]
        base = chunk * hid_rows
        hid[me, pl.ds(base, rows), :] = (gate / (1.0 + jnp.exp(-gate)) * acc_h[:, units:]).astype(BF16)
        plain = acc_s[...]
        turned = pltpu.roll(plain, units // 2, 1)
        low = lax.broadcasted_iota(jnp.int32, plain.shape, 1) < units // 2
        gate = jnp.where(low, plain, turned)
        both = gate / (1.0 + jnp.exp(-gate)) * jnp.where(low, turned, plain)
        top = rows // 2
        packed = jnp.where(low[:top], both[:top], both[top:])
        hid[me, pl.ds(base + rows, top), :] = packed.astype(BF16)
        for way in (CW, CCW):
            hid_copy(chunk, way, 1).start()

    def second_half(chunk):
        window = pl.ds(chunk * rows, rows)
        base = chunk * hid_rows
        top = rows // 2
        both = jnp.concatenate([hid[at, pl.ds(base + rows, top), :] for at in range(n_dp)], axis=1)
        term = jnp.dot(both, dspare[...], preferred_element_type=F32)
        columns = ds_ref.shape[1]
        part[pl.ds(chunk * rows, top), :] = term[:, :columns]
        part[pl.ds(chunk * rows + top, top), :] = term[:, columns:]
        part_copy(chunk).start()
        whole = jnp.concatenate([hid[at, pl.ds(base, rows), :] for at in range(n_dp)], axis=1)
        out_ref[window, pl.ds(0, columns)] = jnp.dot(whole, dh_ref[...], preferred_element_type=F32).astype(BF16)

    def finish(chunk):
        window = pl.ds(chunk * rows, rows)
        part_copy(chunk).wait_recv()
        own = part[window, pl.ds(pl.multiple_of(core * out_half, out_half), out_half)]
        out_ref[window, pl.ds(2 * out_half, out_half)] = (own + pair_part[window, :]).astype(BF16)

    begin(0)
    begin(1)
    zero = jnp.zeros((units // 2, ds_ref.shape[1]), BF16)
    for at in range(n_dp):
        w = ds_ref[pl.ds(at * units // 2, units // 2), :]
        dspare[pl.ds(at * units, units // 2), :] = jnp.concatenate([w, zero], axis=1)
        dspare[pl.ds(at * units + units // 2, units // 2), :] = jnp.concatenate([zero, w], axis=1)

    def arrive(chunk, hop):
        for way in (CW, CCW):
            if hop <= hops(chunk, way):
                feat_copy(chunk, way, hop).wait_recv()
                if hop < hops(chunk, way):
                    feat_copy(chunk, way, hop + 1).start()
                pair_copy(chunk, way, hop).start()

    def hid_arrive(chunk, hop):
        for way in (CW, CCW):
            if hop <= hops(chunk, way):
                hid_copy(chunk, way, hop).wait_recv()
                if hop < hops(chunk, way):
                    hid_copy(chunk, way, hop + 1).start()

    for first in range(0, CHUNKS, 2):
        for hop in range(1, 5):
            for chunk in (first, first + 1):
                arrive(chunk, hop)
                if hop >= 3 and chunk + 2 < CHUNKS and hop == 3:
                    begin(chunk + 2)
                if first >= 2:
                    hid_arrive(chunk - 2, hop)
        for chunk in (first, first + 1):
            if first >= 2:
                second_half(chunk - 2)
            first_half(chunk)
    for hop in range(1, 5):
        for chunk in (CHUNKS - 2, CHUNKS - 1):
            hid_arrive(chunk, hop)
    for chunk in (CHUNKS - 2, CHUNKS - 1):
        second_half(chunk)
    for chunk in range(CHUNKS):
        finish(chunk)
    for chunk in range(CHUNKS):
        for way in (CW, CCW):
            for hop in range(1, hops(chunk, way) + 1):
                feat_copy(chunk, way, hop).wait_send()
                hid_copy(chunk, way, hop).wait_send()
                pair_copy(chunk, way, hop).wait_send()
        pair_copy(chunk, CW, 0).wait_send()
        part_copy(chunk).wait_send()


def experts(rows, wh, ws, dh, ds):
    total, width3 = rows.shape
    n_dp = 8
    width = wh.shape[0] // n_dp
    units = wh.shape[1] // 2
    chunk_rows = total // CHUNKS
    ring_sems = pltpu.SemaphoreType.DMA((CHUNKS, 2, 4))
    pair_sems = pltpu.SemaphoreType.DMA((CHUNKS, 2, 5))
    part_sems = pltpu.SemaphoreType.DMA((CHUNKS,))
    return pl.pallas_call(
        expert_kernel,
        out_shape=jax.ShapeDtypeStruct((total, width3), BF16),
        in_specs=[pl.BlockSpec(memory_space=pltpu.VMEM)] * 5,
        out_specs=pl.BlockSpec(memory_space=pltpu.VMEM),
        scratch_shapes=[
            pltpu.VMEM((n_dp, total, width3), BF16),
            pltpu.VMEM((n_dp, total, width // 2), BF16),
            pltpu.VMEM((n_dp, total + total // 2, units), BF16),
            pltpu.VMEM((chunk_rows, 2 * units), F32),
            pltpu.VMEM((chunk_rows, units), F32),
            pltpu.VMEM((n_dp * units, 2 * width), BF16),
            pltpu.VMEM((total, ds.shape[1]), F32),
            pltpu.VMEM((total, ds.shape[1] // 2), F32),
            ring_sems, ring_sems, pair_sems, pair_sems, ring_sems, ring_sems, part_sems, part_sems,
        ],
        compiler_params=pltpu.CompilerParams(
            collective_id=0, has_side_effects=True, vmem_limit_bytes=56 * 1024 * 1024
        ),
    )(rows, wh, ws, dh, ds)


def route(expert_ids, placement, split_rows, slots, capacity):
    per_group = expert_ids.shape[0] * expert_ids.shape[1]
    chosen = expert_ids.reshape(per_group)
    ordinal = jnp.arange(per_group, dtype=jnp.int32)
    same = (chosen[:, None] == chosen[None, :]) & (ordinal[None, :] < ordinal[:, None])
    rank = jnp.sum(same.astype(jnp.int32), axis=1)
    match = chosen[:, None] == placement[None, :]
    hot = jnp.any(match, axis=1)
    copy = jnp.sum(jnp.where(match, jnp.arange(placement.shape[0], dtype=jnp.int32)[None, :], 0), axis=1)
    split = jnp.sum(jnp.where(match, split_rows[None, :], 0), axis=1)
    moved = hot & (rank >= split)
    slot = jnp.where(moved, slots + copy, chosen)
    position = jnp.where(moved, rank - split, rank)
    return jnp.where(position < capacity, slot * capacity + position, -1).reshape(expert_ids.shape)


def per_device(
    tokens, expert_ids, gate_logits, placement, split_rows,
    gate_up_weight, down_weight, spare_gate_up, spare_down,
):
    n_ep = lax.axis_size("ep")
    spares = placement.shape[0]
    capacity = 8
    width = tokens.shape[1]
    half = width // 2
    table_row = route(expert_ids, placement, split_rows, n_ep, capacity)
    slot_rows = (n_ep + spares) * capacity
    hit = table_row[None] == jnp.arange(slot_rows, dtype=jnp.int32)[:, None, None]
    pick = jnp.any(hit, axis=2).astype(BF16)
    sent = jnp.dot(pick, tokens, preferred_element_type=F32).astype(BF16)
    home = sent[: n_ep * capacity].reshape(n_ep, capacity, width)
    extra = sent[n_ep * capacity :].reshape(spares, capacity, 2, half)
    extra = jnp.transpose(extra, (0, 2, 1, 3)).reshape(n_ep, capacity, half)
    send = jnp.concatenate([home, extra], axis=2)
    rows = lax.all_to_all(send, "ep", split_axis=0, concat_axis=0, tiled=True)
    wh = gate_up_weight[0].reshape(gate_up_weight.shape[1], -1)
    ws = jnp.transpose(spare_gate_up[0], (1, 2, 0)).reshape(-1, spare_gate_up.shape[1])
    out = experts(rows.reshape(n_ep * capacity, width + half), wh, ws, down_weight[0], spare_down[0])
    back = lax.all_to_all(
        out.reshape(n_ep, capacity, width + half), "ep", split_axis=0, concat_axis=0, tiled=True
    ).reshape(n_ep * capacity, width + half)
    score = jax.nn.sigmoid(gate_logits)
    weight = 2.5 * score / jnp.sum(score, axis=1, keepdims=True)
    matrix = jnp.sum(jnp.where(hit, weight[None], 0.0), axis=2).T
    home_matrix = matrix[:, : n_ep * capacity]
    extra_matrix = matrix[:, n_ep * capacity :].reshape(-1, spares, 1, capacity)
    side = jnp.arange(2)[None, :, None, None, None] == jnp.arange(2)[None, None, None, :, None]
    extra_matrix = jnp.where(side, extra_matrix[:, None], 0.0).reshape(-1, n_ep * capacity)

    def exact_dot(a, b):
        high = lax.reduce_precision(a, 8, 7)
        low = (a - high).astype(BF16)
        return jnp.dot(high.astype(BF16), b, preferred_element_type=F32) + jnp.dot(low, b, preferred_element_type=F32)

    mixed = exact_dot(home_matrix, back[:, :width])
    extra = exact_dot(extra_matrix, back[:, width:]).reshape(-1, 2 * half)
    return (mixed + extra).astype(BF16)


def solution(mesh):
    return jax.shard_map(
        per_device,
        mesh=mesh,
        in_specs=(
            P("ep", "dp"),
            P("ep", None),
            P("ep", None),
            P(),
            P(),
            P("ep", None, None, "dp"),
            P("ep", None, "dp"),
            P("ep", None, None, "dp"),
            P("ep", None, "dp"),
        ),
        out_specs=P("ep", "dp"),
        check_vma=False,
    )
```

```python
import functools

import jax
import jax.numpy as jnp
from jax import lax
from jax.experimental import pallas as pl
from jax.experimental.pallas import tpu as pltpu
from jax.sharding import PartitionSpec as P

MESH = pl.DeviceIdType.MESH
F32 = jnp.float32
BF16 = jnp.bfloat16
CHUNKS = 4
CW, CCW = 0, 1


def hops(chunk, way):
    return 4 if chunk % 2 == way else 3


def expert_kernel(
    tokens_ref, pairs_ref, wh_hbm, ws_hbm, dh_hbm, ds_hbm, out_ref,
    tok, tab, tab_sibling, send, mine, feat, pair_feat, hid, acc_h, acc_s, part, pair_part,
    out, back, combine, mix, mix_sibling, wh_ref, ws_ref, dh_ref, ds_ref, dspare,
    ring_send, ring_recv, pair_send, pair_recv, hid_send, hid_recv, part_send, part_recv,
    load_sem, swap_send, swap_recv, go_send, go_recv, own_sem, back_send, back_recv,
):
    n_dp, n_z, n_x = 8, 8, 4
    n_chips = n_z * n_x
    ep = lax.axis_index("ep")
    me = lax.axis_index("dp")
    core = lax.rem(ep, 2)
    chip = ep // 2
    at_x = lax.rem(chip, n_x)
    at_z = chip // n_x
    sibling = {"ep": ep + 1 - 2 * core, "dp": me}
    ring = (
        {"ep": ep, "dp": lax.rem(me + 1, n_dp)},
        {"ep": ep, "dp": lax.rem(me + n_dp - 1, n_dp)},
    )

    def chip_at(dx, dz):
        return lax.rem(at_z + dz, n_z) * n_x + lax.rem(at_x + dx, n_x)

    loads = [
        pltpu.make_async_copy(src, dst, load_sem.at[i])
        for i, (src, dst) in enumerate(
            ((wh_hbm, wh_ref), (ws_hbm, ws_ref), (dh_hbm, dh_ref), (ds_hbm, ds_ref))
        )
    ]
    for load in loads:
        load.start()

    barrier = pltpu.get_barrier_semaphore()
    for other in (sibling, ring[0], ring[1]):
        pl.semaphore_signal(barrier, inc=1, device_id=other, device_id_type=MESH)

    @pl.loop(1, n_chips)
    def _(step):
        other = lax.rem(chip + step, n_chips)
        pl.semaphore_signal(
            barrier, inc=1, device_id={"ep": other * 2 + core, "dp": me}, device_id_type=MESH
        )

    pl.semaphore_wait(barrier, n_chips + 2)

    group = tokens_ref.shape[0]
    width = tokens_ref.shape[1]
    half = width // 2
    block = 16
    rows = n_z * block
    units = wh_ref.shape[1] // 2

    swaps = [
        pltpu.make_async_remote_copy(
            src_ref=src, dst_ref=dst, send_sem=swap_send.at[i], recv_sem=swap_recv.at[i],
            device_id=sibling, device_id_type=MESH,
        )
        for i, (src, dst) in enumerate(
            ((tokens_ref, tok.at[pl.ds(core * group, group)]), (pairs_ref, tab_sibling))
        )
    ]
    for swap in swaps:
        swap.start()
    tok[pl.ds(pl.multiple_of(core * group, group), group), :] = tokens_ref[...]
    for swap in swaps:
        swap.wait_recv()

    both_tables = pairs_ref[...] + tab_sibling[...]
    top_k = pairs_ref.shape[0] // 2
    tab[...] = both_tables
    slot_rows = n_chips * block
    row = lax.broadcasted_iota(jnp.int32, (slot_rows, 2 * group), 0)
    of_group = row % block // 8 * 1024 + row % 8 + 1
    home_key = (of_group + (row // block * 2 + core) * 8).astype(F32)
    spare_key = (of_group + (row // block + 2 * n_chips) * 8).astype(F32)

    def spread(key, weighted):
        found = jnp.zeros(key.shape, F32)
        for k in range(top_k):
            value = tab[top_k + k : top_k + k + 1, :] if weighted else 1.0
            found += jnp.where(tab[k : k + 1, :] == key, value, 0.0)
        return found

    send[:, :width] = jnp.dot(
        spread(home_key, False).astype(BF16), tok[...], preferred_element_type=F32
    ).astype(BF16)
    send[:, width:] = jnp.dot(
        spread(spare_key, False).astype(BF16),
        tok[:, pl.ds(pl.multiple_of(core * half, half), half)],
        preferred_element_type=F32,
    ).astype(BF16)

    def go_copy(dx, dz):
        other = chip_at(dx, dz)
        return pltpu.make_async_remote_copy(
            src_ref=send.at[pl.ds(other * block, block)],
            dst_ref=mine.at[pl.ds((dx * n_z + at_z) * block, block)],
            send_sem=go_send, recv_sem=go_recv.at[dx],
            device_id={"ep": other * 2 + core, "dp": me}, device_id_type=MESH,
        )

    own_go = pltpu.make_async_copy(
        send.at[pl.ds(chip * block, block)], mine.at[pl.ds(at_z * block, block)], own_sem.at[0]
    )
    own_go.start()
    for dx in range(n_x):
        @pl.loop(0 if dx else 1, n_z)
        def _(dz):
            go_copy(dx, dz).start()

    def source(way, hop):
        return lax.rem(me + (n_dp - hop if way == CW else hop), n_dp)

    def feat_copy(chunk, way, hop):
        src = source(way, hop - 1)
        window = pl.ds(chunk * rows, rows)
        return pltpu.make_async_remote_copy(
            src_ref=mine.at[window] if hop == 1 else feat.at[src, window],
            dst_ref=feat.at[src, window],
            send_sem=ring_send.at[chunk, way, hop - 1],
            recv_sem=ring_recv.at[chunk, way, hop - 1],
            device_id=ring[way], device_id_type=MESH,
        )

    def pair_copy(chunk, way, hop):
        src = source(way, hop)
        window = pl.ds(chunk * rows, rows)
        here = mine.at[window, pl.ds(width, half)] if hop == 0 else feat.at[src, window, pl.ds(width, half)]
        return pltpu.make_async_remote_copy(
            src_ref=here,
            dst_ref=pair_feat.at[src, window],
            send_sem=pair_send.at[chunk, way, hop],
            recv_sem=pair_recv.at[chunk, way, hop],
            device_id=sibling, device_id_type=MESH,
        )

    hid_rows = rows + rows // 2

    def hid_copy(chunk, way, hop):
        src = source(way, hop - 1)
        window = pl.ds(chunk * hid_rows, hid_rows)
        return pltpu.make_async_remote_copy(
            src_ref=hid.at[src, window],
            dst_ref=hid.at[src, window],
            send_sem=hid_send.at[chunk, way, hop - 1],
            recv_sem=hid_recv.at[chunk, way, hop - 1],
            device_id=ring[way], device_id_type=MESH,
        )

    columns = ds_ref.shape[1]
    out_half = columns // 2

    def part_copy(chunk):
        window = pl.ds(chunk * rows, rows)
        return pltpu.make_async_remote_copy(
            src_ref=part.at[window, pl.ds((1 - core) * out_half, out_half)],
            dst_ref=pair_part.at[window],
            send_sem=part_send.at[chunk],
            recv_sem=part_recv.at[chunk],
            device_id=sibling, device_id_type=MESH,
        )

    def back_copy(dx, dz):
        z = lax.rem(at_z + dz, n_z)
        other = chip_at(n_x - dx, dz)
        return pltpu.make_async_remote_copy(
            src_ref=out.at[pl.ds((dx * n_z + z) * block, block)],
            dst_ref=back.at[pl.ds(chip * block, block)],
            send_sem=back_send, recv_sem=back_recv,
            device_id={"ep": other * 2 + core, "dp": me}, device_id_type=MESH,
        )

    turned_dims = (((1,), (1,)), ((), ()))

    def spare_term(x, at, side):
        cols = pl.ds(pl.multiple_of(at * width + side * half, half), half)
        return lax.dot_general(x, ws_ref[:, cols], turned_dims, preferred_element_type=F32)

    def project(x, at):
        w = wh_ref[pl.ds(pl.multiple_of(at * width, width), width), :]
        home = jnp.dot(x[:, :width], w, preferred_element_type=F32)
        return home, spare_term(x[:, width:], at, core)

    def begin(chunk):
        window = pl.ds(chunk * rows, rows)
        arrived = mine.at[pl.ds(chunk * rows, rows if chunk else rows - block)]
        pltpu.make_async_copy(arrived, arrived, go_recv.at[chunk]).wait()
        if chunk == 0:
            own_go.wait()
        for way in (CW, CCW):
            feat_copy(chunk, way, 1).start()
        pair_copy(chunk, CW, 0).start()
        if chunk == 0:
            loads[0].wait()
            loads[1].wait()
        acc_h[window, :], acc_s[window, :] = project(mine[window, :], me)

    def add_pair(chunk, way, hop):
        window = pl.ds(chunk * rows, rows)
        src = source(way, hop)
        pair_copy(chunk, way, hop).wait_recv()
        acc_s[window, :] += spare_term(pair_feat[src, window, :], src, 1 - core)

    def arrive(chunk, hop):
        window = pl.ds(chunk * rows, rows)
        ways = [way for way in (CW, CCW) if hop <= hops(chunk, way)]
        for way in ways:
            feat_copy(chunk, way, hop).wait_recv()
            if hop < hops(chunk, way):
                feat_copy(chunk, way, hop + 1).start()
            pair_copy(chunk, way, hop).start()
        for way in ways:
            src = source(way, hop)
            home, spare = project(feat[src, window, :], src)
            acc_h[window, :] += home
            acc_s[window, :] += spare
        if hop == 1:
            add_pair(chunk, CW, 0)
        else:
            for way in (CW, CCW):
                add_pair(chunk, way, hop - 1)

    def first_half(chunk):
        window = pl.ds(chunk * rows, rows)
        for way in (CW, CCW):
            if hops(chunk, way) == 4:
                add_pair(chunk, way, 4)
        gate = acc_h[window, :units]
        base = chunk * hid_rows
        hid[me, pl.ds(base, rows), :] = (gate / (1.0 + jnp.exp(-gate)) * acc_h[window, units:]).astype(BF16)
        plain = acc_s[window, :]
        turned = pltpu.roll(plain, units // 2, 1)
        low = lax.broadcasted_iota(jnp.int32, plain.shape, 1) < units // 2
        gate = jnp.where(low, plain, turned)
        both = gate / (1.0 + jnp.exp(-gate)) * jnp.where(low, turned, plain)
        top = rows // 2
        packed = jnp.where(low[:top], both[:top], both[top:])
        hid[me, pl.ds(base + rows, top), :] = packed.astype(BF16)
        for way in (CW, CCW):
            hid_copy(chunk, way, 1).start()

    def hid_arrive(chunk, hop):
        for way in (CW, CCW):
            if hop <= hops(chunk, way):
                hid_copy(chunk, way, hop).wait_recv()
                if hop < hops(chunk, way):
                    hid_copy(chunk, way, hop + 1).start()

    def second_half(chunk):
        window = pl.ds(chunk * rows, rows)
        base = chunk * hid_rows
        top = rows // 2
        packed = jnp.concatenate([hid[at, pl.ds(base + rows, top), :] for at in range(n_dp)], axis=1)
        low = lax.broadcasted_iota(jnp.int32, packed.shape, 1) % units < units // 2
        none = jnp.zeros_like(packed)
        both = jnp.concatenate([jnp.where(low, packed, none), jnp.where(low, none, packed)], axis=0)
        part[window, :] = jnp.dot(both, dspare[...], preferred_element_type=F32)
        part_copy(chunk).start()
        whole = jnp.concatenate([hid[at, pl.ds(base, rows), :] for at in range(n_dp)], axis=1)
        out[window, :columns] = jnp.dot(whole, dh_ref[...], preferred_element_type=F32).astype(BF16)

    own_back = pltpu.make_async_copy(
        out.at[pl.ds(at_z * block, block)], back.at[pl.ds(chip * block, block)], own_sem.at[1]
    )

    def finish(chunk):
        window = pl.ds(chunk * rows, rows)
        part_copy(chunk).wait_recv()
        own = part[window, pl.ds(pl.multiple_of(core * out_half, out_half), out_half)]
        out[window, columns:] = (own + pair_part[window, :]).astype(BF16)
        if chunk == 0:
            own_back.start()

        @pl.loop(0 if chunk else 1, n_z)
        def _(dz):
            back_copy(chunk, dz).start()

    def prepare():
        for i, key in enumerate((home_key, spare_key)):
            whole = spread(key, True).T
            high = whole.astype(BF16)
            combine[2 * i] = high
            combine[2 * i + 1] = (whole - high.astype(F32)).astype(BF16)
        loads[2].wait()
        loads[3].wait()
        for at in range(n_dp):
            w = ds_ref[pl.ds(at * units // 2, units // 2), :]
            dspare[pl.ds(at * units, units // 2), :] = w
            dspare[pl.ds(at * units + units // 2, units // 2), :] = w

    events = []
    for chunk in range(CHUNKS):
        for hop in range(5):
            events.append((chunk + hop, 0, -chunk, "feat", chunk, hop))
        events.append((chunk + 4, 1, -chunk, "first", chunk, 0))
        for hop in range(1, 5):
            events.append((chunk + 4 + hop, 2, -chunk, "hid", chunk, hop))
        events.append((chunk + 8, 3, -chunk, "second", chunk, 0))
        events.append((chunk + 9, 4, -chunk, "finish", chunk, 0))
    events.append((0, 9, 0, "prepare", 0, 0))
    for _, _, _, kind, chunk, hop in sorted(events):
        if kind == "feat":
            arrive(chunk, hop) if hop else begin(chunk)
        elif kind == "first":
            first_half(chunk)
        elif kind == "hid":
            hid_arrive(chunk, hop)
        elif kind == "second":
            second_half(chunk)
        elif kind == "finish":
            finish(chunk)
        else:
            prepare()

    landed = back.at[pl.ds(0, (n_chips - 1) * block)]
    pltpu.make_async_copy(landed, landed, back_recv).wait()
    own_back.wait()

    def weigh(i, table):
        return jnp.dot(combine[2 * i], table, preferred_element_type=F32) + jnp.dot(
            combine[2 * i + 1], table, preferred_element_type=F32
        )

    mix[...] = weigh(0, back[:, :columns])
    side = pl.ds(pl.multiple_of(core * out_half, out_half), out_half)
    mix[:, side] += weigh(1, back[:, columns:])
    mix_swap = pltpu.make_async_remote_copy(
        src_ref=mix.at[pl.ds((1 - core) * group, group)], dst_ref=mix_sibling,
        send_sem=swap_send.at[2], recv_sem=swap_recv.at[2],
        device_id=sibling, device_id_type=MESH,
    )
    mix_swap.start()
    mix_swap.wait_recv()
    out_ref[...] = (mix[pl.ds(pl.multiple_of(core * group, group), group), :] + mix_sibling[...]).astype(BF16)

    mix_swap.wait_send()
    for swap in swaps:
        swap.wait_send()
    gone = send.at[pl.ds(0, (n_chips - 1) * block)]
    pltpu.make_async_copy(gone, gone, go_send).wait()
    gone = out.at[pl.ds(0, (n_chips - 1) * block)]
    pltpu.make_async_copy(gone, gone, back_send).wait()
    for chunk in range(CHUNKS):
        for way in (CW, CCW):
            for hop in range(1, hops(chunk, way) + 1):
                feat_copy(chunk, way, hop).wait_send()
                hid_copy(chunk, way, hop).wait_send()
                pair_copy(chunk, way, hop).wait_send()
        pair_copy(chunk, CW, 0).wait_send()
        part_copy(chunk).wait_send()


def experts(tokens, pairs, wh, ws, dh, ds):
    group, width = tokens.shape
    n_dp = 8
    half = width // 2
    units = wh.shape[1] // 2
    total = 512
    columns = ds.shape[1]
    lanes = pairs.shape[1]
    dma = pltpu.SemaphoreType.DMA
    ring_sems = dma((CHUNKS, 2, 4))
    pair_sems = dma((CHUNKS, 2, 5))
    part_sems = dma((CHUNKS,))
    in_vmem = pl.BlockSpec(memory_space=pltpu.VMEM)
    in_hbm = pl.BlockSpec(memory_space=pl.ANY)
    return pl.pallas_call(
        expert_kernel,
        out_shape=jax.ShapeDtypeStruct((group, columns), BF16),
        in_specs=[in_vmem] * 2 + [in_hbm] * 4,
        out_specs=in_vmem,
        scratch_shapes=[
            pltpu.VMEM((2 * group, width), BF16),
            pltpu.VMEM(pairs.shape, F32),
            pltpu.VMEM(pairs.shape, F32),
            pltpu.VMEM((total, width + half), BF16),
            pltpu.VMEM((total, width + half), BF16),
            pltpu.VMEM((n_dp, total, width + half), BF16),
            pltpu.VMEM((n_dp, total, half), BF16),
            pltpu.VMEM((n_dp, total + total // 2, units), BF16),
            pltpu.VMEM((total, 2 * units), F32),
            pltpu.VMEM((total, units), F32),
            pltpu.VMEM((total, columns), F32),
            pltpu.VMEM((total, columns // 2), F32),
            pltpu.VMEM((total, columns + columns // 2), BF16),
            pltpu.VMEM((total, columns + columns // 2), BF16),
            pltpu.VMEM((4, lanes, total), BF16),
            pltpu.VMEM((lanes, columns), F32),
            pltpu.VMEM((group, columns), F32),
            pltpu.VMEM(wh.shape, BF16),
            pltpu.VMEM(ws.shape, BF16),
            pltpu.VMEM(dh.shape, BF16),
            pltpu.VMEM(ds.shape, BF16),
            pltpu.VMEM((n_dp * units, columns), BF16),
            ring_sems, ring_sems, pair_sems, pair_sems, ring_sems, ring_sems, part_sems, part_sems,
            dma((4,)), dma((3,)), dma((3,)), dma, dma((4,)), dma((2,)), dma, dma,
        ],
        compiler_params=pltpu.CompilerParams(
            collective_id=0, has_side_effects=True, vmem_limit_bytes=56 * 1024 * 1024
        ),
    )(tokens, pairs, wh, ws, dh, ds)


def route(expert_ids, placement, split_rows, slots, capacity):
    per_group = expert_ids.shape[0] * expert_ids.shape[1]
    chosen = expert_ids.reshape(per_group)
    ordinal = jnp.arange(per_group, dtype=jnp.int32)
    same = (chosen[:, None] == chosen[None, :]) & (ordinal[None, :] < ordinal[:, None])
    rank = jnp.sum(same.astype(jnp.int32), axis=1)
    match = chosen[:, None] == placement[None, :]
    hot = jnp.any(match, axis=1)
    copy = jnp.sum(jnp.where(match, jnp.arange(placement.shape[0], dtype=jnp.int32)[None, :], 0), axis=1)
    split = jnp.sum(jnp.where(match, split_rows[None, :], 0), axis=1)
    moved = hot & (rank >= split)
    slot = jnp.where(moved, slots + copy, chosen)
    position = jnp.where(moved, rank - split, rank)
    return jnp.where(position < capacity, slot * capacity + position, -1).reshape(expert_ids.shape)


def per_device(
    tokens, expert_ids, gate_logits, placement, split_rows,
    gate_up_weight, down_weight, spare_gate_up, spare_down,
):
    n_ep = lax.axis_size("ep")
    core = lax.axis_index("ep") % 2
    table_row = route(expert_ids, placement, split_rows, n_ep, 8).T
    score = jax.nn.sigmoid(gate_logits)
    weight = (2.5 * score / jnp.sum(score, axis=1, keepdims=True)).T
    coded = jnp.where(table_row >= 0, table_row + 1 + 1024 * core, 0).astype(F32)
    pairs = jnp.concatenate([coded, weight], axis=0)
    side = jnp.arange(2)[None, :, None] == core
    pairs = jnp.where(side, pairs[:, None, :], 0.0).reshape(pairs.shape[0], -1)
    wh = gate_up_weight[0].reshape(gate_up_weight.shape[1], -1)
    ws = jnp.transpose(spare_gate_up[0], (1, 2, 0)).reshape(-1, spare_gate_up.shape[1])
    return experts(tokens, pairs, wh, ws, down_weight[0], spare_down[0])


def solution(mesh):
    return jax.shard_map(
        per_device,
        mesh=mesh,
        in_specs=(
            P("ep", "dp"),
            P("ep", None),
            P("ep", None),
            P(),
            P(),
            P("ep", None, None, "dp"),
            P("ep", None, "dp"),
            P("ep", None, None, "dp"),
            P("ep", None, "dp"),
        ),
        out_specs=P("ep", "dp"),
        check_vma=False,
    )
```

```python
import functools

import jax
import jax.numpy as jnp
from jax import lax
from jax.experimental import pallas as pl
from jax.experimental.pallas import tpu as pltpu
from jax.sharding import PartitionSpec as P

MESH = pl.DeviceIdType.MESH
F32 = jnp.float32
BF16 = jnp.bfloat16
CHUNKS = 4
EXTRA = 128
CW, CCW = 0, 1


def hops(chunk, way):
    return 4 if chunk % 2 == way else 3


def expert_kernel(
    tokens_ref, ids_ref, logits_ref, placement_ref, split_ref, wh_hbm, ws_hbm, dh_hbm, ds_hbm, out_ref,
    tok, tab, tab_sibling, tok_extra, send, send_extra, mine, mine_extra, feat, pair_feat, hid, acc_h, acc_s, part, pair_part,
    out, back, combine, mix, mix_sibling, wh_raw, wide, wh_ref, wh_extra, ws_ref, dh_ref, ds_ref, dspare,
    ring_send, ring_recv, pair_send, pair_recv, hid_send, hid_recv, part_send, part_recv,
    load_sem, swap_send, swap_recv, go_send, go_recv, own_sem, back_send, back_recv,
    peer_send, peer_recv, extra_send, extra_recv,
):
    n_dp, n_z, n_x = 8, 8, 4
    n_chips = n_z * n_x
    ep = lax.axis_index("ep")
    me = lax.axis_index("dp")
    core = lax.rem(ep, 2)
    chip = ep // 2
    at_x = lax.rem(chip, n_x)
    at_z = chip // n_x
    sibling = {"ep": ep + 1 - 2 * core, "dp": me}
    ring = (
        {"ep": ep, "dp": lax.rem(me + 1, n_dp)},
        {"ep": ep, "dp": lax.rem(me + n_dp - 1, n_dp)},
    )

    def chip_at(dx, dz):
        return lax.rem(at_z + dz, n_z) * n_x + lax.rem(at_x + dx, n_x)

    loads = [
        pltpu.make_async_copy(src, dst, load_sem.at[i])
        for i, (src, dst) in enumerate(
            ((wh_hbm, wh_raw), (ws_hbm, ws_ref), (dh_hbm, dh_ref), (ds_hbm, ds_ref))
        )
    ]
    for load in loads:
        load.start()

    barrier = pltpu.get_barrier_semaphore()
    pl.semaphore_signal(barrier, inc=1, device_id=sibling, device_id_type=MESH)

    def dp_peer(step):
        return {"ep": ep, "dp": lax.rem(me + step, n_dp)}

    @pl.loop(1, n_dp)
    def _(step):
        pl.semaphore_signal(barrier, inc=1, device_id=dp_peer(step), device_id_type=MESH)

    @pl.loop(1, n_chips)
    def _(step):
        other = lax.rem(chip + step, n_chips)
        pl.semaphore_signal(
            barrier, inc=1, device_id={"ep": other * 2 + core, "dp": me}, device_id_type=MESH
        )

    group = tokens_ref.shape[0]
    width = tokens_ref.shape[1]
    half = width // 2
    lean = width - EXTRA
    block = 16
    rows = n_z * block
    units = dh_hbm.shape[0] // n_dp
    top_k = ids_ref.shape[0]
    experts_ = 2 * n_chips
    lanes = 2 * group
    slot_rows = n_chips * block

    score = 1.0 / (1.0 + jnp.exp(-logits_ref[...]))
    weight = 2.5 * score / jnp.sum(score, axis=0, keepdims=True)
    high = weight.astype(BF16).astype(F32)
    stack = jnp.concatenate([ids_ref[...].astype(F32), high, weight - high], axis=0).astype(BF16)
    place = lax.broadcasted_iota(jnp.int32, (group, lanes), 1) - core * group
    spot = (place == lax.broadcasted_iota(jnp.int32, (group, lanes), 0)).astype(F32).astype(BF16)
    stack = jnp.dot(stack, spot, preferred_element_type=F32)
    row = lax.broadcasted_iota(jnp.int32, (experts_, lanes), 0)
    lane = lax.broadcasted_iota(jnp.int32, (experts_, lanes), 1)
    expert = row % n_chips * 2 + row // n_chips
    here = lane // group == core
    hit = jnp.zeros((experts_, lanes), F32)
    high = jnp.zeros((experts_, lanes), F32)
    rest = jnp.zeros((experts_, lanes), F32)
    for k in range(top_k):
        same = (stack[k : k + 1, :] == expert.astype(F32)) & here
        hit += jnp.where(same, 1.0, 0.0)
        high += jnp.where(same, stack[top_k + k : top_k + k + 1, :], 0.0)
        rest += jnp.where(same, stack[2 * top_k + k : 2 * top_k + k + 1, :], 0.0)
    earlier = lax.broadcasted_iota(jnp.int32, (lanes, lanes), 0) < lax.broadcasted_iota(jnp.int32, (lanes, lanes), 1)
    rank = jnp.dot(hit.astype(BF16), earlier.astype(F32).astype(BF16), preferred_element_type=F32)
    hot = jnp.zeros((experts_, lanes), F32)
    split = jnp.zeros((experts_, lanes), F32)
    spares = placement_ref.shape[0]
    spare_row = lax.broadcasted_iota(jnp.int32, (spares, experts_), 0)
    placed = jnp.zeros((spares, experts_), jnp.int32)
    for r in range(spares):
        chosen = expert == placement_ref[r]
        hot += jnp.where(chosen, 1.0, 0.0)
        split += jnp.where(chosen, split_ref[r].astype(F32), 0.0)
        placed = jnp.where(spare_row == r, placement_ref[r], placed)
    column = lax.broadcasted_iota(jnp.int32, (spares, experts_), 1)
    match = (placed == column % n_chips * 2 + column // n_chips).astype(F32).astype(BF16)
    moved = (hot > 0.0) & (rank >= split)
    capacity = 8.0
    home_code = jnp.where((hit > 0.0) & ~moved & (rank < capacity), rank + 1.0, 0.0)
    over = rank - split
    spare_code = jnp.where((hit > 0.0) & moved & (over < capacity), over + 1.0, 0.0)
    for i, (table, given) in enumerate(((home_code, spare_code), (high, high), (rest, rest))):
        base = i * (experts_ + spares)
        tab[pl.ds(base, experts_), :] = table
        tab[pl.ds(base + experts_, spares), :] = jnp.dot(match, given.astype(BF16), preferred_element_type=F32)

    loads[0].wait()

    @pl.loop(0, n_dp)
    def _(at):
        wide[...] = wh_raw[pl.ds(pl.multiple_of(at * 2 * width, 2 * width), 2 * width), :].astype(F32)
        for j in range(2):
            plain = wide[pl.ds(j, width, stride=2), :].astype(BF16)
            wh_ref[pl.ds(pl.multiple_of(at * lean, EXTRA), lean), j * units : (j + 1) * units] = plain[:lean]
            wh_extra[pl.ds(pl.multiple_of(at * EXTRA, EXTRA), EXTRA), j * units : (j + 1) * units] = plain[lean:]

    pl.semaphore_wait(barrier, n_chips + n_dp - 1)

    own_tokens = pl.ds(pl.multiple_of(core * group, group), group)
    swaps = [
        pltpu.make_async_remote_copy(
            src_ref=src, dst_ref=dst, send_sem=swap_send.at[i], recv_sem=swap_recv.at[i],
            device_id=sibling, device_id_type=MESH,
        )
        for i, (src, dst) in enumerate(((tokens_ref, tok.at[own_tokens]), (tab, tab_sibling)))
    ]
    for swap in swaps:
        swap.start()

    def peer_copy(step):
        return pltpu.make_async_remote_copy(
            src_ref=tokens_ref.at[:, pl.ds(lean, EXTRA)],
            dst_ref=tok_extra.at[me, own_tokens],
            send_sem=peer_send, recv_sem=peer_recv,
            device_id=dp_peer(step), device_id_type=MESH,
        )

    @pl.loop(1, n_dp)
    def _(step):
        peer_copy(step).start()

    tok[own_tokens, :] = tokens_ref[...]
    tok_extra[me, own_tokens, :] = tokens_ref[:, lean:]
    for swap in swaps:
        swap.wait_recv()

    row = lax.broadcasted_iota(jnp.int32, (slot_rows, lanes), 0)
    lane = lax.broadcasted_iota(jnp.int32, (slot_rows, lanes), 1)
    in_group = row % block // 8 == lane // group
    wanted = (row % 8 + 1).astype(F32)

    def spread(i, spare):
        base = i * (experts_ + spares) + (experts_ if spare else core * n_chips)
        window = pl.ds(pl.multiple_of(base, n_chips), n_chips)
        table = tab[window, :] + tab_sibling[window, :]
        return jnp.broadcast_to(table[:, None, :], (n_chips, block, lanes)).reshape(slot_rows, lanes)

    def picked(spare):
        return (spread(0, spare) == wanted) & in_group

    home_pick = picked(False).astype(F32).astype(BF16)
    send[:, :lean] = jnp.dot(home_pick, tok[:, :lean], preferred_element_type=F32).astype(BF16)
    send[:, lean:] = jnp.dot(
        picked(True).astype(F32).astype(BF16),
        tok[:, pl.ds(pl.multiple_of(core * half, half), half)],
        preferred_element_type=F32,
    ).astype(BF16)

    def go_copy(dx, dz):
        other = chip_at(dx, dz)
        return pltpu.make_async_remote_copy(
            src_ref=send.at[pl.ds(other * block, block)],
            dst_ref=mine.at[pl.ds((dx * n_z + at_z) * block, block)],
            send_sem=go_send, recv_sem=go_recv.at[dx],
            device_id={"ep": other * 2 + core, "dp": me}, device_id_type=MESH,
        )

    own_go = pltpu.make_async_copy(
        send.at[pl.ds(chip * block, block)], mine.at[pl.ds(at_z * block, block)], own_sem.at[0]
    )
    own_go.start()
    for dx in range(n_x):
        @pl.loop(0 if dx else 1, n_z)
        def _(dz):
            go_copy(dx, dz).start()

    peers_in = tok_extra.at[pl.ds(0, n_dp - 1), pl.ds(0, group)]
    pltpu.make_async_copy(peers_in, peers_in, peer_recv).wait()
    extra_swap = pltpu.make_async_remote_copy(
        src_ref=tok_extra.at[:, own_tokens], dst_ref=tok_extra.at[:, own_tokens],
        send_sem=swap_send.at[3], recv_sem=swap_recv.at[3], device_id=sibling, device_id_type=MESH,
    )
    extra_swap.start()

    def extra_copy(dx, dz):
        other = chip_at(dx, dz)
        return pltpu.make_async_remote_copy(
            src_ref=send_extra.at[pl.ds(other * block, block)],
            dst_ref=mine_extra.at[pl.ds((dx * n_z + at_z) * block, block)],
            send_sem=extra_send, recv_sem=extra_recv.at[dx],
            device_id={"ep": other * 2 + core, "dp": me}, device_id_type=MESH,
        )

    own_extra = pltpu.make_async_copy(
        send_extra.at[pl.ds(chip * block, block)], mine_extra.at[pl.ds(at_z * block, block)], own_sem.at[2]
    )

    def send_extras():
        extra_swap.wait_recv()
        for at in range(n_dp):
            send_extra[:, at * EXTRA : (at + 1) * EXTRA] = jnp.dot(
                home_pick, tok_extra[at], preferred_element_type=F32
            ).astype(BF16)
        own_extra.start()
        for dx in range(n_x):
            @pl.loop(0 if dx else 1, n_z)
            def _(dz):
                extra_copy(dx, dz).start()

    def source(way, hop):
        return lax.rem(me + (n_dp - hop if way == CW else hop), n_dp)

    def feat_copy(chunk, way, hop):
        src = source(way, hop - 1)
        window = pl.ds(chunk * rows, rows)
        return pltpu.make_async_remote_copy(
            src_ref=mine.at[window] if hop == 1 else feat.at[src, window],
            dst_ref=feat.at[src, window],
            send_sem=ring_send.at[chunk, way, hop - 1],
            recv_sem=ring_recv.at[chunk, way, hop - 1],
            device_id=ring[way], device_id_type=MESH,
        )

    def pair_copy(chunk, way, hop):
        src = source(way, hop)
        window = pl.ds(chunk * rows, rows)
        here = mine.at[window, pl.ds(lean, half)] if hop == 0 else feat.at[src, window, pl.ds(lean, half)]
        return pltpu.make_async_remote_copy(
            src_ref=here,
            dst_ref=pair_feat.at[src, window],
            send_sem=pair_send.at[chunk, way, hop],
            recv_sem=pair_recv.at[chunk, way, hop],
            device_id=sibling, device_id_type=MESH,
        )

    hid_rows = rows + rows // 2

    def hid_copy(chunk, way, hop):
        src = source(way, hop - 1)
        window = pl.ds(chunk * hid_rows, hid_rows)
        return pltpu.make_async_remote_copy(
            src_ref=hid.at[src, window],
            dst_ref=hid.at[src, window],
            send_sem=hid_send.at[chunk, way, hop - 1],
            recv_sem=hid_recv.at[chunk, way, hop - 1],
            device_id=ring[way], device_id_type=MESH,
        )

    columns = ds_ref.shape[1]
    out_half = columns // 2

    def part_copy(chunk):
        window = pl.ds(chunk * rows, rows)
        return pltpu.make_async_remote_copy(
            src_ref=part.at[window, pl.ds((1 - core) * out_half, out_half)],
            dst_ref=pair_part.at[window],
            send_sem=part_send.at[chunk],
            recv_sem=part_recv.at[chunk],
            device_id=sibling, device_id_type=MESH,
        )

    def back_copy(dx, dz):
        z = lax.rem(at_z + dz, n_z)
        other = chip_at(n_x - dx, dz)
        return pltpu.make_async_remote_copy(
            src_ref=out.at[pl.ds((dx * n_z + z) * block, block)],
            dst_ref=back.at[pl.ds(chip * block, block)],
            send_sem=back_send, recv_sem=back_recv,
            device_id={"ep": other * 2 + core, "dp": me}, device_id_type=MESH,
        )

    turned_dims = (((1,), (1,)), ((), ()))

    def spare_term(x, at, side):
        cols = pl.ds(pl.multiple_of(at * width + side * half, half), half)
        return lax.dot_general(x, ws_ref[:, cols], turned_dims, preferred_element_type=F32)

    def project(x, at):
        w = wh_ref[pl.ds(pl.multiple_of(at * lean, EXTRA), lean), :]
        home = jnp.dot(x[:, :lean], w, preferred_element_type=F32)
        return home, spare_term(x[:, lean:], at, core)

    def begin(chunk):
        window = pl.ds(chunk * rows, rows)
        arrived = mine.at[pl.ds(chunk * rows, rows if chunk else rows - block)]
        pltpu.make_async_copy(arrived, arrived, go_recv.at[chunk]).wait()
        if chunk == 0:
            own_go.wait()
        for way in (CW, CCW):
            feat_copy(chunk, way, 1).start()
        pair_copy(chunk, CW, 0).start()
        if chunk == 0:
            loads[1].wait()
        acc_h[window, :], acc_s[window, :] = project(mine[window, :], me)

    def add_pair(chunk, way, hop):
        window = pl.ds(chunk * rows, rows)
        src = source(way, hop)
        pair_copy(chunk, way, hop).wait_recv()
        acc_s[window, :] += spare_term(pair_feat[src, window, :], src, 1 - core)

    def arrive(chunk, hop):
        window = pl.ds(chunk * rows, rows)
        ways = [way for way in (CW, CCW) if hop <= hops(chunk, way)]
        for way in ways:
            feat_copy(chunk, way, hop).wait_recv()
            if hop < hops(chunk, way):
                feat_copy(chunk, way, hop + 1).start()
            pair_copy(chunk, way, hop).start()
        for way in ways:
            src = source(way, hop)
            home, spare = project(feat[src, window, :], src)
            acc_h[window, :] += home
            acc_s[window, :] += spare
        if hop == 1:
            add_pair(chunk, CW, 0)
        else:
            for way in (CW, CCW):
                add_pair(chunk, way, hop - 1)

    def first_half(chunk):
        window = pl.ds(chunk * rows, rows)
        for way in (CW, CCW):
            if hops(chunk, way) == 4:
                add_pair(chunk, way, 4)
        came = mine_extra.at[pl.ds(chunk * rows, rows if chunk else rows - block)]
        pltpu.make_async_copy(came, came, extra_recv.at[chunk]).wait()
        if chunk == 0:
            own_extra.wait()
        acc_h[window, :] += jnp.dot(mine_extra[window, :], wh_extra[...], preferred_element_type=F32)
        gate = acc_h[window, :units]
        base = chunk * hid_rows
        hid[me, pl.ds(base, rows), :] = (gate / (1.0 + jnp.exp(-gate)) * acc_h[window, units:]).astype(BF16)
        plain = acc_s[window, :]
        turned = pltpu.roll(plain, units // 2, 1)
        low = lax.broadcasted_iota(jnp.int32, plain.shape, 1) < units // 2
        gate = jnp.where(low, plain, turned)
        both = gate / (1.0 + jnp.exp(-gate)) * jnp.where(low, turned, plain)
        top = rows // 2
        packed = jnp.where(low[:top], both[:top], both[top:])
        hid[me, pl.ds(base + rows, top), :] = packed.astype(BF16)
        for way in (CW, CCW):
            hid_copy(chunk, way, 1).start()

    def hid_arrive(chunk, hop):
        for way in (CW, CCW):
            if hop <= hops(chunk, way):
                hid_copy(chunk, way, hop).wait_recv()
                if hop < hops(chunk, way):
                    hid_copy(chunk, way, hop + 1).start()

    def second_half(chunk):
        window = pl.ds(chunk * rows, rows)
        base = chunk * hid_rows
        top = rows // 2
        packed = jnp.concatenate([hid[at, pl.ds(base + rows, top), :] for at in range(n_dp)], axis=1)
        low = lax.broadcasted_iota(jnp.int32, packed.shape, 1) % units < units // 2
        none = jnp.zeros_like(packed)
        both = jnp.concatenate([jnp.where(low, packed, none), jnp.where(low, none, packed)], axis=0)
        part[window, :] = jnp.dot(both, dspare[...], preferred_element_type=F32)
        part_copy(chunk).start()
        whole = jnp.concatenate([hid[at, pl.ds(base, rows), :] for at in range(n_dp)], axis=1)
        out[window, :columns] = jnp.dot(whole, dh_ref[...], preferred_element_type=F32).astype(BF16)

    own_back = pltpu.make_async_copy(
        out.at[pl.ds(at_z * block, block)], back.at[pl.ds(chip * block, block)], own_sem.at[1]
    )

    def finish(chunk):
        window = pl.ds(chunk * rows, rows)
        part_copy(chunk).wait_recv()
        own = part[window, pl.ds(pl.multiple_of(core * out_half, out_half), out_half)]
        out[window, columns:] = (own + pair_part[window, :]).astype(BF16)
        if chunk == 0:
            own_back.start()

        @pl.loop(0 if chunk else 1, n_z)
        def _(dz):
            back_copy(chunk, dz).start()

    def prepare():
        for i, spare in enumerate((False, True)):
            for j in range(2):
                combine[2 * i + j] = jnp.where(picked(spare), spread(1 + j, spare), 0.0).T.astype(BF16)
        loads[2].wait()
        loads[3].wait()
        for at in range(n_dp):
            w = ds_ref[pl.ds(at * units // 2, units // 2), :]
            dspare[pl.ds(at * units, units // 2), :] = w
            dspare[pl.ds(at * units + units // 2, units // 2), :] = w

    events = []
    for chunk in range(CHUNKS):
        for hop in range(5):
            events.append((chunk + hop, 0, -chunk, "feat", chunk, hop))
        events.append((chunk + 4, 1, -chunk, "first", chunk, 0))
        for hop in range(1, 5):
            events.append((chunk + 4 + hop, 2, -chunk, "hid", chunk, hop))
        events.append((chunk + 8, 3, -chunk, "second", chunk, 0))
        events.append((chunk + 9, 4, -chunk, "finish", chunk, 0))
    events.append((0, 9, 0, "prepare", 0, 0))
    events.append((0, 0, 9, "extra", 0, 0))
    for _, _, _, kind, chunk, hop in sorted(events):
        if kind == "feat":
            arrive(chunk, hop) if hop else begin(chunk)
        elif kind == "first":
            first_half(chunk)
        elif kind == "hid":
            hid_arrive(chunk, hop)
        elif kind == "second":
            second_half(chunk)
        elif kind == "finish":
            finish(chunk)
        elif kind == "extra":
            send_extras()
        else:
            prepare()

    landed = back.at[pl.ds(0, (n_chips - 1) * block)]
    pltpu.make_async_copy(landed, landed, back_recv).wait()
    own_back.wait()

    def weigh(i, table):
        return jnp.dot(combine[2 * i], table, preferred_element_type=F32) + jnp.dot(
            combine[2 * i + 1], table, preferred_element_type=F32
        )

    mix[...] = weigh(0, back[:, :columns])
    side = pl.ds(pl.multiple_of(core * out_half, out_half), out_half)
    mix[:, side] += weigh(1, back[:, columns:])
    mix_swap = pltpu.make_async_remote_copy(
        src_ref=mix.at[pl.ds((1 - core) * group, group)], dst_ref=mix_sibling,
        send_sem=swap_send.at[2], recv_sem=swap_recv.at[2],
        device_id=sibling, device_id_type=MESH,
    )
    mix_swap.start()
    mix_swap.wait_recv()
    out_ref[...] = (mix[pl.ds(pl.multiple_of(core * group, group), group), :] + mix_sibling[...]).astype(BF16)

    mix_swap.wait_send()
    extra_swap.wait_send()
    pltpu.make_async_copy(peers_in, peers_in, peer_send).wait()
    gone = send_extra.at[pl.ds(0, (n_chips - 1) * block)]
    pltpu.make_async_copy(gone, gone, extra_send).wait()
    for swap in swaps:
        swap.wait_send()
    gone = send.at[pl.ds(0, (n_chips - 1) * block)]
    pltpu.make_async_copy(gone, gone, go_send).wait()
    gone = out.at[pl.ds(0, (n_chips - 1) * block)]
    pltpu.make_async_copy(gone, gone, back_send).wait()
    for chunk in range(CHUNKS):
        for way in (CW, CCW):
            for hop in range(1, hops(chunk, way) + 1):
                feat_copy(chunk, way, hop).wait_send()
                hid_copy(chunk, way, hop).wait_send()
                pair_copy(chunk, way, hop).wait_send()
        pair_copy(chunk, CW, 0).wait_send()
        part_copy(chunk).wait_send()


def experts(tokens, ids, logits, placement, split_rows, wh, ws, dh, ds):
    group, width = tokens.shape
    n_dp = 8
    half = width // 2
    lean = width - EXTRA
    units = wh.shape[1]
    total = 512
    columns = ds.shape[1]
    lanes = 2 * group
    table_rows = 3 * (64 + placement.shape[0])
    dma = pltpu.SemaphoreType.DMA
    ring_sems = dma((CHUNKS, 2, 4))
    pair_sems = dma((CHUNKS, 2, 5))
    part_sems = dma((CHUNKS,))
    in_vmem = pl.BlockSpec(memory_space=pltpu.VMEM)
    in_smem = pl.BlockSpec(memory_space=pltpu.SMEM)
    in_hbm = pl.BlockSpec(memory_space=pl.ANY)
    return pl.pallas_call(
        expert_kernel,
        out_shape=jax.ShapeDtypeStruct((group, columns), BF16),
        in_specs=[in_vmem] * 3 + [in_smem] * 2 + [in_hbm] * 4,
        out_specs=in_vmem,
        scratch_shapes=[
            pltpu.VMEM((lanes, width), BF16),
            pltpu.VMEM((table_rows, lanes), F32),
            pltpu.VMEM((table_rows, lanes), F32),
            pltpu.VMEM((n_dp, lanes, EXTRA), BF16),
            pltpu.VMEM((total, lean + half), BF16),
            pltpu.VMEM((total, n_dp * EXTRA), BF16),
            pltpu.VMEM((total, lean + half), BF16),
            pltpu.VMEM((total, n_dp * EXTRA), BF16),
            pltpu.VMEM((n_dp, total, lean + half), BF16),
            pltpu.VMEM((n_dp, total, half), BF16),
            pltpu.VMEM((n_dp, total + total // 2, units), BF16),
            pltpu.VMEM((total, 2 * units), F32),
            pltpu.VMEM((total, units), F32),
            pltpu.VMEM((total, columns), F32),
            pltpu.VMEM((total, columns // 2), F32),
            pltpu.VMEM((total, columns + columns // 2), BF16),
            pltpu.VMEM((total, columns + columns // 2), BF16),
            pltpu.VMEM((4, lanes, total), BF16),
            pltpu.VMEM((lanes, columns), F32),
            pltpu.VMEM((group, columns), F32),
            pltpu.VMEM(wh.shape, BF16),
            pltpu.VMEM((2 * width, units), F32),
            pltpu.VMEM((n_dp * lean, 2 * units), BF16),
            pltpu.VMEM((n_dp * EXTRA, 2 * units), BF16),
            pltpu.VMEM(ws.shape, BF16),
            pltpu.VMEM(dh.shape, BF16),
            pltpu.VMEM(ds.shape, BF16),
            pltpu.VMEM((n_dp * units, columns), BF16),
            ring_sems, ring_sems, pair_sems, pair_sems, ring_sems, ring_sems, part_sems, part_sems,
            dma((4,)), dma((4,)), dma((4,)), dma, dma((4,)), dma((3,)), dma, dma,
            dma, dma, dma, dma((4,)),
        ],
        compiler_params=pltpu.CompilerParams(
            collective_id=0, has_side_effects=True, vmem_limit_bytes=56 * 1024 * 1024
        ),
    )(tokens, ids, logits, placement, split_rows, wh, ws, dh, ds)


def per_device(
    tokens, expert_ids, gate_logits, placement, split_rows,
    gate_up_weight, down_weight, spare_gate_up, spare_down,
):
    wh = gate_up_weight.reshape(-1, gate_up_weight.shape[3])
    ws = jnp.transpose(spare_gate_up[0], (1, 2, 0)).reshape(-1, spare_gate_up.shape[1])
    return experts(
        tokens, expert_ids.T, gate_logits.T, placement, split_rows, wh, ws, down_weight[0], spare_down[0]
    )


def solution(mesh):
    return jax.shard_map(
        per_device,
        mesh=mesh,
        in_specs=(
            P("ep", "dp"),
            P("ep", None),
            P("ep", None),
            P(),
            P(),
            P("ep", None, None, "dp"),
            P("ep", None, "dp"),
            P("ep", None, None, "dp"),
            P("ep", None, "dp"),
        ),
        out_specs=P("ep", "dp"),
        check_vma=False,
    )
```

```python
import functools

import jax
import jax.numpy as jnp
from jax import lax
from jax.experimental import pallas as pl
from jax.experimental.pallas import tpu as pltpu
from jax.sharding import PartitionSpec as P

MESH = pl.DeviceIdType.MESH
F32 = jnp.float32
BF16 = jnp.bfloat16
CHUNKS = 4
PART = 128
EXTRA = 2 * PART


def parts(chunk):
    return 1 if chunk < 2 else 2
CW, CCW = 0, 1


def hops(chunk, way):
    return 4 if chunk % 2 == way else 3


def expert_kernel(
    tokens_ref, ids_ref, logits_ref, placement_ref, split_ref, wh_hbm, ws_hbm, dh_hbm, ds_hbm, out_ref,
    tok, tab, tab_sibling, tok_extra, send, send_extra, mine, mine_extra, feat, pair_feat, hid, acc_h, acc_s, part, pair_part,
    out, back, combine, mix, mix_sibling, wh_raw, wide, wh_ref, wh_extra, ws_ref, dh_ref, ds_ref, dspare,
    ring_send, ring_recv, pair_send, pair_recv, hid_send, hid_recv, part_send, part_recv,
    load_sem, swap_send, swap_recv, go_send, go_recv, own_sem, back_send, back_recv,
    peer_send, peer_recv, extra_send, extra_recv,
):
    n_dp, n_z, n_x = 8, 8, 4
    n_chips = n_z * n_x
    ep = lax.axis_index("ep")
    me = lax.axis_index("dp")
    core = lax.rem(ep, 2)
    chip = ep // 2
    at_x = lax.rem(chip, n_x)
    at_z = chip // n_x
    sibling = {"ep": ep + 1 - 2 * core, "dp": me}
    ring = (
        {"ep": ep, "dp": lax.rem(me + 1, n_dp)},
        {"ep": ep, "dp": lax.rem(me + n_dp - 1, n_dp)},
    )

    def chip_at(dx, dz):
        return lax.rem(at_z + dz, n_z) * n_x + lax.rem(at_x + dx, n_x)

    loads = [
        pltpu.make_async_copy(src, dst, load_sem.at[i])
        for i, (src, dst) in enumerate(
            ((wh_hbm, wh_raw), (ws_hbm, ws_ref), (dh_hbm, dh_ref), (ds_hbm, ds_ref))
        )
    ]
    for load in loads:
        load.start()

    barrier = pltpu.get_barrier_semaphore()
    pl.semaphore_signal(barrier, inc=1, device_id=sibling, device_id_type=MESH)

    def dp_peer(step):
        return {"ep": ep, "dp": lax.rem(me + step, n_dp)}

    @pl.loop(1, n_dp)
    def _(step):
        pl.semaphore_signal(barrier, inc=1, device_id=dp_peer(step), device_id_type=MESH)

    @pl.loop(1, n_chips)
    def _(step):
        other = lax.rem(chip + step, n_chips)
        pl.semaphore_signal(
            barrier, inc=1, device_id={"ep": other * 2 + core, "dp": me}, device_id_type=MESH
        )

    group = tokens_ref.shape[0]
    width = tokens_ref.shape[1]
    half = width // 2
    block = 16

    def home_width(chunk):
        return width - parts(chunk) * PART

    def ring_width(chunk):
        return half + home_width(chunk)

    def extra_width(chunk):
        return parts(chunk) * n_dp * PART

    rows = n_z * block
    units = dh_hbm.shape[0] // n_dp
    top_k = ids_ref.shape[0]
    experts_ = 2 * n_chips
    lanes = 2 * group
    slot_rows = n_chips * block

    score = 1.0 / (1.0 + jnp.exp(-logits_ref[...]))
    weight = 2.5 * score / jnp.sum(score, axis=0, keepdims=True)
    high = weight.astype(BF16).astype(F32)
    stack = jnp.concatenate([ids_ref[...].astype(F32), high, weight - high], axis=0).astype(BF16)
    place = lax.broadcasted_iota(jnp.int32, (group, lanes), 1) - core * group
    spot = (place == lax.broadcasted_iota(jnp.int32, (group, lanes), 0)).astype(F32).astype(BF16)
    stack = jnp.dot(stack, spot, preferred_element_type=F32)
    row = lax.broadcasted_iota(jnp.int32, (experts_, lanes), 0)
    lane = lax.broadcasted_iota(jnp.int32, (experts_, lanes), 1)
    expert = row % n_chips * 2 + row // n_chips
    here = lane // group == core
    hit = jnp.zeros((experts_, lanes), F32)
    high = jnp.zeros((experts_, lanes), F32)
    rest = jnp.zeros((experts_, lanes), F32)
    for k in range(top_k):
        same = (stack[k : k + 1, :] == expert.astype(F32)) & here
        hit += jnp.where(same, 1.0, 0.0)
        high += jnp.where(same, stack[top_k + k : top_k + k + 1, :], 0.0)
        rest += jnp.where(same, stack[2 * top_k + k : 2 * top_k + k + 1, :], 0.0)
    earlier = lax.broadcasted_iota(jnp.int32, (lanes, lanes), 0) < lax.broadcasted_iota(jnp.int32, (lanes, lanes), 1)
    rank = jnp.dot(hit.astype(BF16), earlier.astype(F32).astype(BF16), preferred_element_type=F32)
    hot = jnp.zeros((experts_, lanes), F32)
    split = jnp.zeros((experts_, lanes), F32)
    spares = placement_ref.shape[0]
    spare_row = lax.broadcasted_iota(jnp.int32, (spares, experts_), 0)
    placed = jnp.zeros((spares, experts_), jnp.int32)
    for r in range(spares):
        chosen = expert == placement_ref[r]
        hot += jnp.where(chosen, 1.0, 0.0)
        split += jnp.where(chosen, split_ref[r].astype(F32), 0.0)
        placed = jnp.where(spare_row == r, placement_ref[r], placed)
    column = lax.broadcasted_iota(jnp.int32, (spares, experts_), 1)
    match = (placed == column % n_chips * 2 + column // n_chips).astype(F32).astype(BF16)
    moved = (hot > 0.0) & (rank >= split)
    capacity = 8.0
    home_code = jnp.where((hit > 0.0) & ~moved & (rank < capacity), rank + 1.0, 0.0)
    over = rank - split
    spare_code = jnp.where((hit > 0.0) & moved & (over < capacity), over + 1.0, 0.0)
    for i, (table, given) in enumerate(((home_code, spare_code), (high, high), (rest, rest))):
        base = i * (experts_ + spares)
        tab[pl.ds(base, experts_), :] = table
        tab[pl.ds(base + experts_, spares), :] = jnp.dot(match, given.astype(BF16), preferred_element_type=F32)

    loads[0].wait()

    @pl.loop(0, n_dp)
    def _(at):
        wide[...] = wh_raw[pl.ds(pl.multiple_of(at * 2 * width, 2 * width), 2 * width), :].astype(F32)
        for j in range(2):
            plain = wide[pl.ds(j, width, stride=2), :].astype(BF16)
            wh_ref[pl.ds(pl.multiple_of(at * width, width), width), j * units : (j + 1) * units] = plain
            for part_at in range(2):
                end = width - part_at * PART
                wh_extra[part_at, pl.ds(pl.multiple_of(at * PART, PART), PART), j * units : (j + 1) * units] = (
                    plain[end - PART : end]
                )

    pl.semaphore_wait(barrier, n_chips + n_dp - 1)

    own_tokens = pl.ds(pl.multiple_of(core * group, group), group)
    swaps = [
        pltpu.make_async_remote_copy(
            src_ref=src, dst_ref=dst, send_sem=swap_send.at[i], recv_sem=swap_recv.at[i],
            device_id=sibling, device_id_type=MESH,
        )
        for i, (src, dst) in enumerate(((tokens_ref, tok.at[own_tokens]), (tab, tab_sibling)))
    ]
    for swap in swaps:
        swap.start()

    def peer_copy(step):
        return pltpu.make_async_remote_copy(
            src_ref=tokens_ref.at[:, pl.ds(width - EXTRA, EXTRA)],
            dst_ref=tok_extra.at[me, own_tokens],
            send_sem=peer_send, recv_sem=peer_recv,
            device_id=dp_peer(step), device_id_type=MESH,
        )

    @pl.loop(1, n_dp)
    def _(step):
        peer_copy(step).start()

    tok[own_tokens, :] = tokens_ref[...]
    tok_extra[me, own_tokens, :] = tokens_ref[:, width - EXTRA :]
    for swap in swaps:
        swap.wait_recv()

    row = lax.broadcasted_iota(jnp.int32, (slot_rows, lanes), 0)
    lane = lax.broadcasted_iota(jnp.int32, (slot_rows, lanes), 1)
    in_group = row % block // 8 == lane // group
    wanted = (row % 8 + 1).astype(F32)

    def spread(i, spare):
        base = i * (experts_ + spares) + (experts_ if spare else core * n_chips)
        window = pl.ds(pl.multiple_of(base, n_chips), n_chips)
        table = tab[window, :] + tab_sibling[window, :]
        return jnp.broadcast_to(table[:, None, :], (n_chips, block, lanes)).reshape(slot_rows, lanes)

    def picked(spare):
        return (spread(0, spare) == wanted) & in_group

    home_pick = picked(False).astype(F32).astype(BF16)
    widest = home_width(0)
    send[:, half:] = jnp.dot(home_pick, tok[:, :widest], preferred_element_type=F32).astype(BF16)
    send[:, :half] = jnp.dot(
        picked(True).astype(F32).astype(BF16),
        tok[:, pl.ds(pl.multiple_of(core * half, half), half)],
        preferred_element_type=F32,
    ).astype(BF16)

    def go_copy(dx, dz):
        other = chip_at(dx, dz)
        return pltpu.make_async_remote_copy(
            src_ref=send.at[pl.ds(other * block, block), pl.ds(0, ring_width(dx))],
            dst_ref=mine.at[pl.ds((dx * n_z + at_z) * block, block), pl.ds(0, ring_width(dx))],
            send_sem=go_send.at[dx], recv_sem=go_recv.at[dx],
            device_id={"ep": other * 2 + core, "dp": me}, device_id_type=MESH,
        )

    own_go = pltpu.make_async_copy(
        send.at[pl.ds(chip * block, block), pl.ds(0, ring_width(0))],
        mine.at[pl.ds(at_z * block, block), pl.ds(0, ring_width(0))],
        own_sem.at[0],
    )
    own_go.start()
    for dx in range(n_x):
        @pl.loop(0 if dx else 1, n_z)
        def _(dz):
            go_copy(dx, dz).start()

    peers_in = tok_extra.at[pl.ds(0, n_dp - 1), pl.ds(0, group)]
    extra_swap = pltpu.make_async_remote_copy(
        src_ref=tok_extra.at[:, own_tokens], dst_ref=tok_extra.at[:, own_tokens],
        send_sem=swap_send.at[3], recv_sem=swap_recv.at[3], device_id=sibling, device_id_type=MESH,
    )

    def swap_extras():
        pltpu.make_async_copy(peers_in, peers_in, peer_recv).wait()
        extra_swap.start()

    def extra_copy(dx, dz):
        other = chip_at(dx, dz)
        return pltpu.make_async_remote_copy(
            src_ref=send_extra.at[pl.ds(other * block, block), pl.ds(0, extra_width(dx))],
            dst_ref=mine_extra.at[pl.ds((dx * n_z + at_z) * block, block), pl.ds(0, extra_width(dx))],
            send_sem=extra_send.at[dx], recv_sem=extra_recv.at[dx],
            device_id={"ep": other * 2 + core, "dp": me}, device_id_type=MESH,
        )

    own_extra = pltpu.make_async_copy(
        send_extra.at[pl.ds(chip * block, block), pl.ds(0, extra_width(0))],
        mine_extra.at[pl.ds(at_z * block, block), pl.ds(0, extra_width(0))],
        own_sem.at[2],
    )

    def send_extras():
        extra_swap.wait_recv()
        for at in range(n_dp):
            both = jnp.dot(home_pick, tok_extra[at], preferred_element_type=F32).astype(BF16)
            send_extra[:, at * PART : (at + 1) * PART] = both[:, PART:]
            send_extra[:, (n_dp + at) * PART : (n_dp + at + 1) * PART] = both[:, :PART]
        own_extra.start()
        for dx in range(n_x):
            @pl.loop(0 if dx else 1, n_z)
            def _(dz):
                extra_copy(dx, dz).start()

    def source(way, hop):
        return lax.rem(me + (n_dp - hop if way == CW else hop), n_dp)

    def feat_copy(chunk, way, hop):
        src = source(way, hop - 1)
        window = pl.ds(chunk * rows, rows)
        cols = pl.ds(0, ring_width(chunk))
        return pltpu.make_async_remote_copy(
            src_ref=mine.at[window, cols] if hop == 1 else feat.at[src, window, cols],
            dst_ref=feat.at[src, window, cols],
            send_sem=ring_send.at[chunk, way, hop - 1],
            recv_sem=ring_recv.at[chunk, way, hop - 1],
            device_id=ring[way], device_id_type=MESH,
        )

    def pair_copy(chunk, way, hop):
        src = source(way, hop)
        window = pl.ds(chunk * rows, rows)
        here = mine.at[window, pl.ds(0, half)] if hop == 0 else feat.at[src, window, pl.ds(0, half)]
        return pltpu.make_async_remote_copy(
            src_ref=here,
            dst_ref=pair_feat.at[src, window],
            send_sem=pair_send.at[chunk, way, hop],
            recv_sem=pair_recv.at[chunk, way, hop],
            device_id=sibling, device_id_type=MESH,
        )

    hid_rows = rows + rows // 2

    def hid_copy(chunk, way, hop):
        src = source(way, hop - 1)
        window = pl.ds(chunk * hid_rows, hid_rows)
        return pltpu.make_async_remote_copy(
            src_ref=hid.at[src, window],
            dst_ref=hid.at[src, window],
            send_sem=hid_send.at[chunk, way, hop - 1],
            recv_sem=hid_recv.at[chunk, way, hop - 1],
            device_id=ring[way], device_id_type=MESH,
        )

    columns = ds_ref.shape[1]
    out_half = columns // 2

    def part_copy(chunk):
        window = pl.ds(chunk * rows, rows)
        return pltpu.make_async_remote_copy(
            src_ref=part.at[window, pl.ds((1 - core) * out_half, out_half)],
            dst_ref=pair_part.at[window],
            send_sem=part_send.at[chunk],
            recv_sem=part_recv.at[chunk],
            device_id=sibling, device_id_type=MESH,
        )

    def back_copy(dx, dz):
        z = lax.rem(at_z + dz, n_z)
        other = chip_at(n_x - dx, dz)
        return pltpu.make_async_remote_copy(
            src_ref=out.at[pl.ds((dx * n_z + z) * block, block)],
            dst_ref=back.at[pl.ds(chip * block, block)],
            send_sem=back_send, recv_sem=back_recv,
            device_id={"ep": other * 2 + core, "dp": me}, device_id_type=MESH,
        )

    turned_dims = (((1,), (1,)), ((), ()))

    def spare_term(x, at, side):
        cols = pl.ds(pl.multiple_of(at * width + side * half, half), half)
        return lax.dot_general(x, ws_ref[:, cols], turned_dims, preferred_element_type=F32)

    def project(x, at):
        depth = x.shape[1] - half
        w = wh_ref[pl.ds(pl.multiple_of(at * width, width), depth), :]
        home = jnp.dot(x[:, half:], w, preferred_element_type=F32)
        return home, spare_term(x[:, :half], at, core)

    def begin(chunk):
        window = pl.ds(chunk * rows, rows)
        arrived = mine.at[pl.ds(chunk * rows, rows if chunk else rows - block), pl.ds(0, ring_width(chunk))]
        pltpu.make_async_copy(arrived, arrived, go_recv.at[chunk]).wait()
        if chunk == 0:
            own_go.wait()
        for way in (CW, CCW):
            feat_copy(chunk, way, 1).start()
        pair_copy(chunk, CW, 0).start()
        if chunk == 0:
            loads[1].wait()
        acc_h[window, :], acc_s[window, :] = project(mine[window, : ring_width(chunk)], me)

    def add_pair(chunk, way, hop):
        window = pl.ds(chunk * rows, rows)
        src = source(way, hop)
        pair_copy(chunk, way, hop).wait_recv()
        acc_s[window, :] += spare_term(pair_feat[src, window, :], src, 1 - core)

    def arrive(chunk, hop):
        window = pl.ds(chunk * rows, rows)
        ways = [way for way in (CW, CCW) if hop <= hops(chunk, way)]
        for way in ways:
            feat_copy(chunk, way, hop).wait_recv()
            if hop < hops(chunk, way):
                feat_copy(chunk, way, hop + 1).start()
            pair_copy(chunk, way, hop).start()
        for way in ways:
            src = source(way, hop)
            home, spare = project(feat[src, window, : ring_width(chunk)], src)
            acc_h[window, :] += home
            acc_s[window, :] += spare
        if hop == 1:
            add_pair(chunk, CW, 0)
        else:
            for way in (CW, CCW):
                add_pair(chunk, way, hop - 1)

    def first_half(chunk):
        window = pl.ds(chunk * rows, rows)
        for way in (CW, CCW):
            if hops(chunk, way) == 4:
                add_pair(chunk, way, 4)
        came = mine_extra.at[pl.ds(chunk * rows, rows if chunk else rows - block), pl.ds(0, extra_width(chunk))]
        pltpu.make_async_copy(came, came, extra_recv.at[chunk]).wait()
        if chunk == 0:
            own_extra.wait()
        for part_at in range(parts(chunk)):
            x = mine_extra[window, part_at * n_dp * PART : (part_at + 1) * n_dp * PART]
            acc_h[window, :] += jnp.dot(x, wh_extra[part_at], preferred_element_type=F32)
        gate = acc_h[window, :units]
        base = chunk * hid_rows
        hid[me, pl.ds(base, rows), :] = (gate / (1.0 + jnp.exp(-gate)) * acc_h[window, units:]).astype(BF16)
        plain = acc_s[window, :]
        turned = pltpu.roll(plain, units // 2, 1)
        low = lax.broadcasted_iota(jnp.int32, plain.shape, 1) < units // 2
        gate = jnp.where(low, plain, turned)
        both = gate / (1.0 + jnp.exp(-gate)) * jnp.where(low, turned, plain)
        top = rows // 2
        packed = jnp.where(low[:top], both[:top], both[top:])
        hid[me, pl.ds(base + rows, top), :] = packed.astype(BF16)
        for way in (CW, CCW):
            hid_copy(chunk, way, 1).start()

    def hid_arrive(chunk, hop):
        for way in (CW, CCW):
            if hop <= hops(chunk, way):
                hid_copy(chunk, way, hop).wait_recv()
                if hop < hops(chunk, way):
                    hid_copy(chunk, way, hop + 1).start()

    def second_half(chunk):
        window = pl.ds(chunk * rows, rows)
        base = chunk * hid_rows
        top = rows // 2
        packed = jnp.concatenate([hid[at, pl.ds(base + rows, top), :] for at in range(n_dp)], axis=1)
        low = lax.broadcasted_iota(jnp.int32, packed.shape, 1) % units < units // 2
        none = jnp.zeros_like(packed)
        both = jnp.concatenate([jnp.where(low, packed, none), jnp.where(low, none, packed)], axis=0)
        part[window, :] = jnp.dot(both, dspare[...], preferred_element_type=F32)
        part_copy(chunk).start()
        whole = jnp.concatenate([hid[at, pl.ds(base, rows), :] for at in range(n_dp)], axis=1)
        out[window, :columns] = jnp.dot(whole, dh_ref[...], preferred_element_type=F32).astype(BF16)

    own_back = pltpu.make_async_copy(
        out.at[pl.ds(at_z * block, block)], back.at[pl.ds(chip * block, block)], own_sem.at[1]
    )

    def finish(chunk):
        window = pl.ds(chunk * rows, rows)
        part_copy(chunk).wait_recv()
        own = part[window, pl.ds(pl.multiple_of(core * out_half, out_half), out_half)]
        out[window, columns:] = (own + pair_part[window, :]).astype(BF16)
        if chunk == 0:
            own_back.start()

        @pl.loop(0 if chunk else 1, n_z)
        def _(dz):
            back_copy(chunk, dz).start()

    def prepare():
        for i, spare in enumerate((False, True)):
            for j in range(2):
                combine[2 * i + j] = jnp.where(picked(spare), spread(1 + j, spare), 0.0).T.astype(BF16)
        loads[2].wait()
        loads[3].wait()
        for at in range(n_dp):
            w = ds_ref[pl.ds(at * units // 2, units // 2), :]
            dspare[pl.ds(at * units, units // 2), :] = w
            dspare[pl.ds(at * units + units // 2, units // 2), :] = w

    events = []
    for chunk in range(CHUNKS):
        for hop in range(5):
            events.append((chunk + hop, 0, -chunk, "feat", chunk, hop))
        events.append((chunk + 4, 1, -chunk, "first", chunk, 0))
        for hop in range(1, 5):
            events.append((chunk + 4 + hop, 2, -chunk, "hid", chunk, hop))
        events.append((chunk + 8, 3, -chunk, "second", chunk, 0))
        events.append((chunk + 9, 4, -chunk, "finish", chunk, 0))
    events.append((0, 9, 0, "prepare", 0, 0))
    events.append((0, 0, 9, "peers", 0, 0))
    events.append((1, 0, -0.5, "extra", 0, 0))
    for _, _, _, kind, chunk, hop in sorted(events):
        if kind == "feat":
            arrive(chunk, hop) if hop else begin(chunk)
        elif kind == "first":
            first_half(chunk)
        elif kind == "hid":
            hid_arrive(chunk, hop)
        elif kind == "second":
            second_half(chunk)
        elif kind == "finish":
            finish(chunk)
        elif kind == "extra":
            send_extras()
        elif kind == "peers":
            swap_extras()
        else:
            prepare()

    landed = back.at[pl.ds(0, (n_chips - 1) * block)]
    pltpu.make_async_copy(landed, landed, back_recv).wait()
    own_back.wait()

    def weigh(i, table):
        return jnp.dot(combine[2 * i], table, preferred_element_type=F32) + jnp.dot(
            combine[2 * i + 1], table, preferred_element_type=F32
        )

    mix[...] = weigh(0, back[:, :columns])
    side = pl.ds(pl.multiple_of(core * out_half, out_half), out_half)
    mix[:, side] += weigh(1, back[:, columns:])
    mix_swap = pltpu.make_async_remote_copy(
        src_ref=mix.at[pl.ds((1 - core) * group, group)], dst_ref=mix_sibling,
        send_sem=swap_send.at[2], recv_sem=swap_recv.at[2],
        device_id=sibling, device_id_type=MESH,
    )
    mix_swap.start()
    mix_swap.wait_recv()
    out_ref[...] = (mix[pl.ds(pl.multiple_of(core * group, group), group), :] + mix_sibling[...]).astype(BF16)

    mix_swap.wait_send()
    extra_swap.wait_send()
    pltpu.make_async_copy(peers_in, peers_in, peer_send).wait()
    for chunk in range(CHUNKS):
        count = rows if chunk else rows - block
        gone = send_extra.at[pl.ds(0, count), pl.ds(0, extra_width(chunk))]
        pltpu.make_async_copy(gone, gone, extra_send.at[chunk]).wait()
        gone = send.at[pl.ds(0, count), pl.ds(0, ring_width(chunk))]
        pltpu.make_async_copy(gone, gone, go_send.at[chunk]).wait()
    for swap in swaps:
        swap.wait_send()
    gone = out.at[pl.ds(0, (n_chips - 1) * block)]
    pltpu.make_async_copy(gone, gone, back_send).wait()
    for chunk in range(CHUNKS):
        for way in (CW, CCW):
            for hop in range(1, hops(chunk, way) + 1):
                feat_copy(chunk, way, hop).wait_send()
                hid_copy(chunk, way, hop).wait_send()
                pair_copy(chunk, way, hop).wait_send()
        pair_copy(chunk, CW, 0).wait_send()
        part_copy(chunk).wait_send()


def experts(tokens, ids, logits, placement, split_rows, wh, ws, dh, ds):
    group, width = tokens.shape
    n_dp = 8
    half = width // 2
    lean = width - PART
    units = wh.shape[1]
    total = 512
    columns = ds.shape[1]
    lanes = 2 * group
    table_rows = 3 * (64 + placement.shape[0])
    dma = pltpu.SemaphoreType.DMA
    ring_sems = dma((CHUNKS, 2, 4))
    pair_sems = dma((CHUNKS, 2, 5))
    part_sems = dma((CHUNKS,))
    in_vmem = pl.BlockSpec(memory_space=pltpu.VMEM)
    in_smem = pl.BlockSpec(memory_space=pltpu.SMEM)
    in_hbm = pl.BlockSpec(memory_space=pl.ANY)
    return pl.pallas_call(
        expert_kernel,
        out_shape=jax.ShapeDtypeStruct((group, columns), BF16),
        in_specs=[in_vmem] * 3 + [in_smem] * 2 + [in_hbm] * 4,
        out_specs=in_vmem,
        scratch_shapes=[
            pltpu.VMEM((lanes, width), BF16),
            pltpu.VMEM((table_rows, lanes), F32),
            pltpu.VMEM((table_rows, lanes), F32),
            pltpu.VMEM((n_dp, lanes, EXTRA), BF16),
            pltpu.VMEM((total, lean + half), BF16),
            pltpu.VMEM((total, n_dp * EXTRA), BF16),
            pltpu.VMEM((total, lean + half), BF16),
            pltpu.VMEM((total, n_dp * EXTRA), BF16),
            pltpu.VMEM((n_dp, total, lean + half), BF16),
            pltpu.VMEM((n_dp, total, half), BF16),
            pltpu.VMEM((n_dp, total + total // 2, units), BF16),
            pltpu.VMEM((total, 2 * units), F32),
            pltpu.VMEM((total, units), F32),
            pltpu.VMEM((total, columns), F32),
            pltpu.VMEM((total, columns // 2), F32),
            pltpu.VMEM((total, columns + columns // 2), BF16),
            pltpu.VMEM((total, columns + columns // 2), BF16),
            pltpu.VMEM((4, lanes, total), BF16),
            pltpu.VMEM((lanes, columns), F32),
            pltpu.VMEM((group, columns), F32),
            pltpu.VMEM(wh.shape, BF16),
            pltpu.VMEM((2 * width, units), F32),
            pltpu.VMEM((n_dp * width, 2 * units), BF16),
            pltpu.VMEM((2, n_dp * PART, 2 * units), BF16),
            pltpu.VMEM(ws.shape, BF16),
            pltpu.VMEM(dh.shape, BF16),
            pltpu.VMEM(ds.shape, BF16),
            pltpu.VMEM((n_dp * units, columns), BF16),
            ring_sems, ring_sems, pair_sems, pair_sems, ring_sems, ring_sems, part_sems, part_sems,
            dma((4,)), dma((4,)), dma((4,)), dma((4,)), dma((4,)), dma((3,)), dma, dma,
            dma, dma, dma((4,)), dma((4,)),
        ],
        compiler_params=pltpu.CompilerParams(
            collective_id=0, has_side_effects=True, vmem_limit_bytes=56 * 1024 * 1024
        ),
    )(tokens, ids, logits, placement, split_rows, wh, ws, dh, ds)


def per_device(
    tokens, expert_ids, gate_logits, placement, split_rows,
    gate_up_weight, down_weight, spare_gate_up, spare_down,
):
    wh = gate_up_weight.reshape(-1, gate_up_weight.shape[3])
    ws = jnp.transpose(spare_gate_up[0], (1, 2, 0)).reshape(-1, spare_gate_up.shape[1])
    return experts(
        tokens, expert_ids.T, gate_logits.T, placement, split_rows, wh, ws, down_weight[0], spare_down[0]
    )


def solution(mesh):
    return jax.shard_map(
        per_device,
        mesh=mesh,
        in_specs=(
            P("ep", "dp"),
            P("ep", None),
            P("ep", None),
            P(),
            P(),
            P("ep", None, None, "dp"),
            P("ep", None, "dp"),
            P("ep", None, None, "dp"),
            P("ep", None, "dp"),
        ),
        out_specs=P("ep", "dp"),
        check_vma=False,
    )
```

```python
import functools

import jax
import jax.numpy as jnp
from jax import lax
from jax.experimental import pallas as pl
from jax.experimental.pallas import tpu as pltpu
from jax.sharding import PartitionSpec as P

MESH = pl.DeviceIdType.MESH
F32 = jnp.float32
BF16 = jnp.bfloat16
CHUNKS = 4
PART = 128
EXTRA = 2 * PART


def parts(chunk):
    return 1 if chunk < 1 else 2
CW, CCW = 0, 1


def hops(chunk, way):
    return 4 if chunk % 2 == way else 3


def expert_kernel(
    tokens_ref, ids_ref, logits_ref, placement_ref, split_ref, wh_hbm, ws_hbm, dh_hbm, ds_hbm, out_ref,
    tok, tab, tab_sibling, tok_extra, send, send_extra, mine, mine_extra, feat, pair_feat, hid, acc_h, acc_s, part, pair_part,
    out, back, combine, mix, mix_sibling, wh_raw, wide, wh_ref, wh_extra, ws_ref, dh_ref, ds_ref, dspare,
    ring_send, ring_recv, pair_send, pair_recv, hid_send, hid_recv, part_send, part_recv,
    load_sem, swap_send, swap_recv, go_send, go_recv, own_sem, back_send, back_recv,
    peer_send, peer_recv, extra_send, extra_recv,
):
    n_dp, n_z, n_x = 8, 8, 4
    n_chips = n_z * n_x
    ep = lax.axis_index("ep")
    me = lax.axis_index("dp")
    core = lax.rem(ep, 2)
    chip = ep // 2
    at_x = lax.rem(chip, n_x)
    at_z = chip // n_x
    sibling = {"ep": ep + 1 - 2 * core, "dp": me}
    ring = (
        {"ep": ep, "dp": lax.rem(me + 1, n_dp)},
        {"ep": ep, "dp": lax.rem(me + n_dp - 1, n_dp)},
    )

    def chip_at(dx, dz):
        return lax.rem(at_z + dz, n_z) * n_x + lax.rem(at_x + dx, n_x)

    loads = [
        pltpu.make_async_copy(src, dst, load_sem.at[i])
        for i, (src, dst) in enumerate(
            ((wh_hbm, wh_raw), (ws_hbm, ws_ref), (dh_hbm, dh_ref), (ds_hbm, ds_ref))
        )
    ]
    for load in loads:
        load.start()

    barrier = pltpu.get_barrier_semaphore()
    pl.semaphore_signal(barrier, inc=1, device_id=sibling, device_id_type=MESH)

    def dp_peer(step):
        return {"ep": ep, "dp": lax.rem(me + step, n_dp)}

    @pl.loop(1, n_dp)
    def _(step):
        pl.semaphore_signal(barrier, inc=1, device_id=dp_peer(step), device_id_type=MESH)

    @pl.loop(1, n_chips)
    def _(step):
        other = lax.rem(chip + step, n_chips)
        pl.semaphore_signal(
            barrier, inc=1, device_id={"ep": other * 2 + core, "dp": me}, device_id_type=MESH
        )

    group = tokens_ref.shape[0]
    width = tokens_ref.shape[1]
    half = width // 2
    block = 16

    def home_width(chunk):
        return width - parts(chunk) * PART

    def ring_width(chunk):
        return half + home_width(chunk)

    def extra_width(chunk):
        return parts(chunk) * n_dp * PART

    rows = n_z * block
    units = dh_hbm.shape[0] // n_dp
    top_k = ids_ref.shape[0]
    experts_ = 2 * n_chips
    lanes = 2 * group
    slot_rows = n_chips * block

    score = 1.0 / (1.0 + jnp.exp(-logits_ref[...]))
    weight = 2.5 * score / jnp.sum(score, axis=0, keepdims=True)
    high = weight.astype(BF16).astype(F32)
    stack = jnp.concatenate([ids_ref[...].astype(F32), high, weight - high], axis=0).astype(BF16)
    place = lax.broadcasted_iota(jnp.int32, (group, lanes), 1) - core * group
    spot = (place == lax.broadcasted_iota(jnp.int32, (group, lanes), 0)).astype(F32).astype(BF16)
    stack = jnp.dot(stack, spot, preferred_element_type=F32)
    row = lax.broadcasted_iota(jnp.int32, (experts_, lanes), 0)
    lane = lax.broadcasted_iota(jnp.int32, (experts_, lanes), 1)
    expert = row % n_chips * 2 + row // n_chips
    here = lane // group == core
    hit = jnp.zeros((experts_, lanes), F32)
    high = jnp.zeros((experts_, lanes), F32)
    rest = jnp.zeros((experts_, lanes), F32)
    for k in range(top_k):
        same = (stack[k : k + 1, :] == expert.astype(F32)) & here
        hit += jnp.where(same, 1.0, 0.0)
        high += jnp.where(same, stack[top_k + k : top_k + k + 1, :], 0.0)
        rest += jnp.where(same, stack[2 * top_k + k : 2 * top_k + k + 1, :], 0.0)
    earlier = lax.broadcasted_iota(jnp.int32, (lanes, lanes), 0) < lax.broadcasted_iota(jnp.int32, (lanes, lanes), 1)
    rank = jnp.dot(hit.astype(BF16), earlier.astype(F32).astype(BF16), preferred_element_type=F32)
    hot = jnp.zeros((experts_, lanes), F32)
    split = jnp.zeros((experts_, lanes), F32)
    spares = placement_ref.shape[0]
    spare_row = lax.broadcasted_iota(jnp.int32, (spares, experts_), 0)
    placed = jnp.zeros((spares, experts_), jnp.int32)
    for r in range(spares):
        chosen = expert == placement_ref[r]
        hot += jnp.where(chosen, 1.0, 0.0)
        split += jnp.where(chosen, split_ref[r].astype(F32), 0.0)
        placed = jnp.where(spare_row == r, placement_ref[r], placed)
    column = lax.broadcasted_iota(jnp.int32, (spares, experts_), 1)
    match = (placed == column % n_chips * 2 + column // n_chips).astype(F32).astype(BF16)
    moved = (hot > 0.0) & (rank >= split)
    capacity = 8.0
    home_code = jnp.where((hit > 0.0) & ~moved & (rank < capacity), rank + 1.0, 0.0)
    over = rank - split
    spare_code = jnp.where((hit > 0.0) & moved & (over < capacity), over + 1.0, 0.0)
    for i, (table, given) in enumerate(((home_code, spare_code), (high, high), (rest, rest))):
        base = i * (experts_ + spares)
        tab[pl.ds(base, experts_), :] = table
        tab[pl.ds(base + experts_, spares), :] = jnp.dot(match, given.astype(BF16), preferred_element_type=F32)

    loads[0].wait()

    @pl.loop(0, n_dp)
    def _(at):
        wide[...] = wh_raw[pl.ds(pl.multiple_of(at * 2 * width, 2 * width), 2 * width), :].astype(F32)
        for j in range(2):
            plain = wide[pl.ds(j, width, stride=2), :].astype(BF16)
            wh_ref[pl.ds(pl.multiple_of(at * width, width), width), j * units : (j + 1) * units] = plain
            for part_at in range(2):
                end = width - part_at * PART
                wh_extra[part_at, pl.ds(pl.multiple_of(at * PART, PART), PART), j * units : (j + 1) * units] = (
                    plain[end - PART : end]
                )

    pl.semaphore_wait(barrier, n_chips + n_dp - 1)

    own_tokens = pl.ds(pl.multiple_of(core * group, group), group)
    swaps = [
        pltpu.make_async_remote_copy(
            src_ref=src, dst_ref=dst, send_sem=swap_send.at[i], recv_sem=swap_recv.at[i],
            device_id=sibling, device_id_type=MESH,
        )
        for i, (src, dst) in enumerate(((tokens_ref, tok.at[own_tokens]), (tab, tab_sibling)))
    ]
    for swap in swaps:
        swap.start()

    def peer_copy(step):
        return pltpu.make_async_remote_copy(
            src_ref=tokens_ref.at[:, pl.ds(width - EXTRA, EXTRA)],
            dst_ref=tok_extra.at[me, own_tokens],
            send_sem=peer_send, recv_sem=peer_recv,
            device_id=dp_peer(step), device_id_type=MESH,
        )

    @pl.loop(1, n_dp)
    def _(step):
        peer_copy(step).start()

    tok[own_tokens, :] = tokens_ref[...]
    tok_extra[me, own_tokens, :] = tokens_ref[:, width - EXTRA :]
    for swap in swaps:
        swap.wait_recv()

    row = lax.broadcasted_iota(jnp.int32, (slot_rows, lanes), 0)
    lane = lax.broadcasted_iota(jnp.int32, (slot_rows, lanes), 1)
    in_group = row % block // 8 == lane // group
    wanted = (row % 8 + 1).astype(F32)

    def spread(i, spare):
        base = i * (experts_ + spares) + (experts_ if spare else core * n_chips)
        window = pl.ds(pl.multiple_of(base, n_chips), n_chips)
        table = tab[window, :] + tab_sibling[window, :]
        return jnp.broadcast_to(table[:, None, :], (n_chips, block, lanes)).reshape(slot_rows, lanes)

    def picked(spare):
        return (spread(0, spare) == wanted) & in_group

    home_pick = picked(False).astype(F32).astype(BF16)
    widest = home_width(0)
    send[:, half:] = jnp.dot(home_pick, tok[:, :widest], preferred_element_type=F32).astype(BF16)
    send[:, :half] = jnp.dot(
        picked(True).astype(F32).astype(BF16),
        tok[:, pl.ds(pl.multiple_of(core * half, half), half)],
        preferred_element_type=F32,
    ).astype(BF16)

    def go_copy(dx, dz):
        other = chip_at(dx, dz)
        return pltpu.make_async_remote_copy(
            src_ref=send.at[pl.ds(other * block, block), pl.ds(0, ring_width(dx))],
            dst_ref=mine.at[pl.ds((dx * n_z + at_z) * block, block), pl.ds(0, ring_width(dx))],
            send_sem=go_send.at[dx], recv_sem=go_recv.at[dx],
            device_id={"ep": other * 2 + core, "dp": me}, device_id_type=MESH,
        )

    own_go = pltpu.make_async_copy(
        send.at[pl.ds(chip * block, block), pl.ds(0, ring_width(0))],
        mine.at[pl.ds(at_z * block, block), pl.ds(0, ring_width(0))],
        own_sem.at[0],
    )
    own_go.start()
    for dx in range(n_x):
        @pl.loop(0 if dx else 1, n_z)
        def _(dz):
            go_copy(dx, dz).start()

    peers_in = tok_extra.at[pl.ds(0, n_dp - 1), pl.ds(0, group)]
    extra_swap = pltpu.make_async_remote_copy(
        src_ref=tok_extra.at[:, own_tokens], dst_ref=tok_extra.at[:, own_tokens],
        send_sem=swap_send.at[3], recv_sem=swap_recv.at[3], device_id=sibling, device_id_type=MESH,
    )

    def swap_extras():
        pltpu.make_async_copy(peers_in, peers_in, peer_recv).wait()
        extra_swap.start()

    def extra_copy(dx, dz):
        other = chip_at(dx, dz)
        return pltpu.make_async_remote_copy(
            src_ref=send_extra.at[pl.ds(other * block, block), pl.ds(0, extra_width(dx))],
            dst_ref=mine_extra.at[pl.ds((dx * n_z + at_z) * block, block), pl.ds(0, extra_width(dx))],
            send_sem=extra_send.at[dx], recv_sem=extra_recv.at[dx],
            device_id={"ep": other * 2 + core, "dp": me}, device_id_type=MESH,
        )

    own_extra = pltpu.make_async_copy(
        send_extra.at[pl.ds(chip * block, block), pl.ds(0, extra_width(0))],
        mine_extra.at[pl.ds(at_z * block, block), pl.ds(0, extra_width(0))],
        own_sem.at[2],
    )

    def send_extras():
        extra_swap.wait_recv()
        for at in range(n_dp):
            both = jnp.dot(home_pick, tok_extra[at], preferred_element_type=F32).astype(BF16)
            send_extra[:, at * PART : (at + 1) * PART] = both[:, PART:]
            send_extra[:, (n_dp + at) * PART : (n_dp + at + 1) * PART] = both[:, :PART]
        own_extra.start()
        for dx in range(n_x):
            @pl.loop(0 if dx else 1, n_z)
            def _(dz):
                extra_copy(dx, dz).start()

    def source(way, hop):
        return lax.rem(me + (n_dp - hop if way == CW else hop), n_dp)

    def feat_copy(chunk, way, hop):
        src = source(way, hop - 1)
        window = pl.ds(chunk * rows, rows)
        cols = pl.ds(0, ring_width(chunk))
        return pltpu.make_async_remote_copy(
            src_ref=mine.at[window, cols] if hop == 1 else feat.at[src, window, cols],
            dst_ref=feat.at[src, window, cols],
            send_sem=ring_send.at[chunk, way, hop - 1],
            recv_sem=ring_recv.at[chunk, way, hop - 1],
            device_id=ring[way], device_id_type=MESH,
        )

    def pair_copy(chunk, way, hop):
        src = source(way, hop)
        window = pl.ds(chunk * rows, rows)
        here = mine.at[window, pl.ds(0, half)] if hop == 0 else feat.at[src, window, pl.ds(0, half)]
        return pltpu.make_async_remote_copy(
            src_ref=here,
            dst_ref=pair_feat.at[src, window],
            send_sem=pair_send.at[chunk, way, hop],
            recv_sem=pair_recv.at[chunk, way, hop],
            device_id=sibling, device_id_type=MESH,
        )

    hid_rows = rows + rows // 2

    def hid_copy(chunk, way, hop):
        src = source(way, hop - 1)
        window = pl.ds(chunk * hid_rows, hid_rows)
        return pltpu.make_async_remote_copy(
            src_ref=hid.at[src, window],
            dst_ref=hid.at[src, window],
            send_sem=hid_send.at[chunk, way, hop - 1],
            recv_sem=hid_recv.at[chunk, way, hop - 1],
            device_id=ring[way], device_id_type=MESH,
        )

    columns = ds_ref.shape[1]
    out_half = columns // 2

    def part_copy(chunk):
        window = pl.ds(chunk * rows, rows)
        return pltpu.make_async_remote_copy(
            src_ref=part.at[window, pl.ds((1 - core) * out_half, out_half)],
            dst_ref=pair_part.at[window],
            send_sem=part_send.at[chunk],
            recv_sem=part_recv.at[chunk],
            device_id=sibling, device_id_type=MESH,
        )

    def back_copy(dx, dz):
        z = lax.rem(at_z + dz, n_z)
        other = chip_at(n_x - dx, dz)
        return pltpu.make_async_remote_copy(
            src_ref=out.at[pl.ds((dx * n_z + z) * block, block)],
            dst_ref=back.at[pl.ds(chip * block, block)],
            send_sem=back_send, recv_sem=back_recv,
            device_id={"ep": other * 2 + core, "dp": me}, device_id_type=MESH,
        )

    turned_dims = (((1,), (1,)), ((), ()))

    def spare_term(x, at, side):
        cols = pl.ds(pl.multiple_of(at * width + side * half, half), half)
        return lax.dot_general(x, ws_ref[:, cols], turned_dims, preferred_element_type=F32)

    def project(x, at):
        depth = x.shape[1] - half
        w = wh_ref[pl.ds(pl.multiple_of(at * width, width), depth), :]
        home = jnp.dot(x[:, half:], w, preferred_element_type=F32)
        return home, spare_term(x[:, :half], at, core)

    def begin(chunk):
        window = pl.ds(chunk * rows, rows)
        arrived = mine.at[pl.ds(chunk * rows, rows if chunk else rows - block), pl.ds(0, ring_width(chunk))]
        pltpu.make_async_copy(arrived, arrived, go_recv.at[chunk]).wait()
        if chunk == 0:
            own_go.wait()
        for way in (CW, CCW):
            feat_copy(chunk, way, 1).start()
        pair_copy(chunk, CW, 0).start()
        if chunk == 0:
            loads[1].wait()
        acc_h[window, :], acc_s[window, :] = project(mine[window, : ring_width(chunk)], me)

    def add_pair(chunk, way, hop):
        window = pl.ds(chunk * rows, rows)
        src = source(way, hop)
        pair_copy(chunk, way, hop).wait_recv()
        acc_s[window, :] += spare_term(pair_feat[src, window, :], src, 1 - core)

    def arrive(chunk, hop):
        window = pl.ds(chunk * rows, rows)
        ways = [way for way in (CW, CCW) if hop <= hops(chunk, way)]
        for way in ways:
            feat_copy(chunk, way, hop).wait_recv()
            if hop < hops(chunk, way):
                feat_copy(chunk, way, hop + 1).start()
            pair_copy(chunk, way, hop).start()
        for way in ways:
            src = source(way, hop)
            home, spare = project(feat[src, window, : ring_width(chunk)], src)
            acc_h[window, :] += home
            acc_s[window, :] += spare
        if hop == 1:
            add_pair(chunk, CW, 0)
        else:
            for way in (CW, CCW):
                add_pair(chunk, way, hop - 1)

    def first_half(chunk):
        window = pl.ds(chunk * rows, rows)
        for way in (CW, CCW):
            if hops(chunk, way) == 4:
                add_pair(chunk, way, 4)
        came = mine_extra.at[pl.ds(chunk * rows, rows if chunk else rows - block), pl.ds(0, extra_width(chunk))]
        pltpu.make_async_copy(came, came, extra_recv.at[chunk]).wait()
        if chunk == 0:
            own_extra.wait()
        for part_at in range(parts(chunk)):
            x = mine_extra[window, part_at * n_dp * PART : (part_at + 1) * n_dp * PART]
            acc_h[window, :] += jnp.dot(x, wh_extra[part_at], preferred_element_type=F32)
        gate = acc_h[window, :units]
        base = chunk * hid_rows
        hid[me, pl.ds(base, rows), :] = (gate / (1.0 + jnp.exp(-gate)) * acc_h[window, units:]).astype(BF16)
        plain = acc_s[window, :]
        turned = pltpu.roll(plain, units // 2, 1)
        low = lax.broadcasted_iota(jnp.int32, plain.shape, 1) < units // 2
        gate = jnp.where(low, plain, turned)
        both = gate / (1.0 + jnp.exp(-gate)) * jnp.where(low, turned, plain)
        top = rows // 2
        packed = jnp.where(low[:top], both[:top], both[top:])
        hid[me, pl.ds(base + rows, top), :] = packed.astype(BF16)
        for way in (CW, CCW):
            hid_copy(chunk, way, 1).start()

    def hid_arrive(chunk, hop):
        for way in (CW, CCW):
            if hop <= hops(chunk, way):
                hid_copy(chunk, way, hop).wait_recv()
                if hop < hops(chunk, way):
                    hid_copy(chunk, way, hop + 1).start()

    def second_half(chunk):
        window = pl.ds(chunk * rows, rows)
        base = chunk * hid_rows
        top = rows // 2
        packed = jnp.concatenate([hid[at, pl.ds(base + rows, top), :] for at in range(n_dp)], axis=1)
        low = lax.broadcasted_iota(jnp.int32, packed.shape, 1) % units < units // 2
        none = jnp.zeros_like(packed)
        both = jnp.concatenate([jnp.where(low, packed, none), jnp.where(low, none, packed)], axis=0)
        part[window, :] = jnp.dot(both, dspare[...], preferred_element_type=F32)
        part_copy(chunk).start()
        whole = jnp.concatenate([hid[at, pl.ds(base, rows), :] for at in range(n_dp)], axis=1)
        out[window, :columns] = jnp.dot(whole, dh_ref[...], preferred_element_type=F32).astype(BF16)

    own_back = pltpu.make_async_copy(
        out.at[pl.ds(at_z * block, block)], back.at[pl.ds(chip * block, block)], own_sem.at[1]
    )

    def finish(chunk):
        window = pl.ds(chunk * rows, rows)
        part_copy(chunk).wait_recv()
        own = part[window, pl.ds(pl.multiple_of(core * out_half, out_half), out_half)]
        out[window, columns:] = (own + pair_part[window, :]).astype(BF16)
        if chunk == 0:
            own_back.start()

        @pl.loop(0 if chunk else 1, n_z)
        def _(dz):
            back_copy(chunk, dz).start()

    def prepare():
        for i, spare in enumerate((False, True)):
            for j in range(2):
                combine[2 * i + j] = jnp.where(picked(spare), spread(1 + j, spare), 0.0).T.astype(BF16)
        loads[2].wait()
        loads[3].wait()
        for at in range(n_dp):
            w = ds_ref[pl.ds(at * units // 2, units // 2), :]
            dspare[pl.ds(at * units, units // 2), :] = w
            dspare[pl.ds(at * units + units // 2, units // 2), :] = w

    events = []
    for chunk in range(CHUNKS):
        for hop in range(5):
            events.append((chunk + hop, 0, -chunk, "feat", chunk, hop))
        events.append((chunk + 4, 1, -chunk, "first", chunk, 0))
        for hop in range(1, 5):
            events.append((chunk + 4 + hop, 2, -chunk, "hid", chunk, hop))
        events.append((chunk + 8, 3, -chunk, "second", chunk, 0))
        events.append((chunk + 9, 4, -chunk, "finish", chunk, 0))
    events.append((0, 9, 0, "prepare", 0, 0))
    events.append((0, 0, 9, "peers", 0, 0))
    events.append((0, 0, 10, "extra", 0, 0))
    for _, _, _, kind, chunk, hop in sorted(events):
        if kind == "feat":
            arrive(chunk, hop) if hop else begin(chunk)
        elif kind == "first":
            first_half(chunk)
        elif kind == "hid":
            hid_arrive(chunk, hop)
        elif kind == "second":
            second_half(chunk)
        elif kind == "finish":
            finish(chunk)
        elif kind == "extra":
            send_extras()
        elif kind == "peers":
            swap_extras()
        else:
            prepare()

    landed = back.at[pl.ds(0, (n_chips - 1) * block)]
    pltpu.make_async_copy(landed, landed, back_recv).wait()
    own_back.wait()

    def weigh(i, table):
        return jnp.dot(combine[2 * i], table, preferred_element_type=F32) + jnp.dot(
            combine[2 * i + 1], table, preferred_element_type=F32
        )

    mix[...] = weigh(0, back[:, :columns])
    side = pl.ds(pl.multiple_of(core * out_half, out_half), out_half)
    mix[:, side] += weigh(1, back[:, columns:])
    mix_swap = pltpu.make_async_remote_copy(
        src_ref=mix.at[pl.ds((1 - core) * group, group)], dst_ref=mix_sibling,
        send_sem=swap_send.at[2], recv_sem=swap_recv.at[2],
        device_id=sibling, device_id_type=MESH,
    )
    mix_swap.start()
    mix_swap.wait_recv()
    out_ref[...] = (mix[pl.ds(pl.multiple_of(core * group, group), group), :] + mix_sibling[...]).astype(BF16)

    mix_swap.wait_send()
    extra_swap.wait_send()
    pltpu.make_async_copy(peers_in, peers_in, peer_send).wait()
    for chunk in range(CHUNKS):
        count = rows if chunk else rows - block
        gone = send_extra.at[pl.ds(0, count), pl.ds(0, extra_width(chunk))]
        pltpu.make_async_copy(gone, gone, extra_send.at[chunk]).wait()
        gone = send.at[pl.ds(0, count), pl.ds(0, ring_width(chunk))]
        pltpu.make_async_copy(gone, gone, go_send.at[chunk]).wait()
    for swap in swaps:
        swap.wait_send()
    gone = out.at[pl.ds(0, (n_chips - 1) * block)]
    pltpu.make_async_copy(gone, gone, back_send).wait()
    for chunk in range(CHUNKS):
        for way in (CW, CCW):
            for hop in range(1, hops(chunk, way) + 1):
                feat_copy(chunk, way, hop).wait_send()
                hid_copy(chunk, way, hop).wait_send()
                pair_copy(chunk, way, hop).wait_send()
        pair_copy(chunk, CW, 0).wait_send()
        part_copy(chunk).wait_send()


def experts(tokens, ids, logits, placement, split_rows, wh, ws, dh, ds):
    group, width = tokens.shape
    n_dp = 8
    half = width // 2
    lean = width - PART
    units = wh.shape[1]
    total = 512
    columns = ds.shape[1]
    lanes = 2 * group
    table_rows = 3 * (64 + placement.shape[0])
    dma = pltpu.SemaphoreType.DMA
    ring_sems = dma((CHUNKS, 2, 4))
    pair_sems = dma((CHUNKS, 2, 5))
    part_sems = dma((CHUNKS,))
    in_vmem = pl.BlockSpec(memory_space=pltpu.VMEM)
    in_smem = pl.BlockSpec(memory_space=pltpu.SMEM)
    in_hbm = pl.BlockSpec(memory_space=pl.ANY)
    return pl.pallas_call(
        expert_kernel,
        out_shape=jax.ShapeDtypeStruct((group, columns), BF16),
        in_specs=[in_vmem] * 3 + [in_smem] * 2 + [in_hbm] * 4,
        out_specs=in_vmem,
        scratch_shapes=[
            pltpu.VMEM((lanes, width), BF16),
            pltpu.VMEM((table_rows, lanes), F32),
            pltpu.VMEM((table_rows, lanes), F32),
            pltpu.VMEM((n_dp, lanes, EXTRA), BF16),
            pltpu.VMEM((total, lean + half), BF16),
            pltpu.VMEM((total, n_dp * EXTRA), BF16),
            pltpu.VMEM((total, lean + half), BF16),
            pltpu.VMEM((total, n_dp * EXTRA), BF16),
            pltpu.VMEM((n_dp, total, lean + half), BF16),
            pltpu.VMEM((n_dp, total, half), BF16),
            pltpu.VMEM((n_dp, total + total // 2, units), BF16),
            pltpu.VMEM((total, 2 * units), F32),
            pltpu.VMEM((total, units), F32),
            pltpu.VMEM((total, columns), F32),
            pltpu.VMEM((total, columns // 2), F32),
            pltpu.VMEM((total, columns + columns // 2), BF16),
            pltpu.VMEM((total, columns + columns // 2), BF16),
            pltpu.VMEM((4, lanes, total), BF16),
            pltpu.VMEM((lanes, columns), F32),
            pltpu.VMEM((group, columns), F32),
            pltpu.VMEM(wh.shape, BF16),
            pltpu.VMEM((2 * width, units), F32),
            pltpu.VMEM((n_dp * width, 2 * units), BF16),
            pltpu.VMEM((2, n_dp * PART, 2 * units), BF16),
            pltpu.VMEM(ws.shape, BF16),
            pltpu.VMEM(dh.shape, BF16),
            pltpu.VMEM(ds.shape, BF16),
            pltpu.VMEM((n_dp * units, columns), BF16),
            ring_sems, ring_sems, pair_sems, pair_sems, ring_sems, ring_sems, part_sems, part_sems,
            dma((4,)), dma((4,)), dma((4,)), dma((4,)), dma((4,)), dma((3,)), dma, dma,
            dma, dma, dma((4,)), dma((4,)),
        ],
        compiler_params=pltpu.CompilerParams(
            collective_id=0, has_side_effects=True, vmem_limit_bytes=56 * 1024 * 1024
        ),
    )(tokens, ids, logits, placement, split_rows, wh, ws, dh, ds)


def per_device(
    tokens, expert_ids, gate_logits, placement, split_rows,
    gate_up_weight, down_weight, spare_gate_up, spare_down,
):
    wh = gate_up_weight.reshape(-1, gate_up_weight.shape[3])
    ws = jnp.transpose(spare_gate_up[0], (1, 2, 0)).reshape(-1, spare_gate_up.shape[1])
    return experts(
        tokens, expert_ids.T, gate_logits.T, placement, split_rows, wh, ws, down_weight[0], spare_down[0]
    )


def solution(mesh):
    return jax.shard_map(
        per_device,
        mesh=mesh,
        in_specs=(
            P("ep", "dp"),
            P("ep", None),
            P("ep", None),
            P(),
            P(),
            P("ep", None, None, "dp"),
            P("ep", None, "dp"),
            P("ep", None, None, "dp"),
            P("ep", None, "dp"),
        ),
        out_specs=P("ep", "dp"),
        check_vma=False,
    )
```

```python
import functools

import jax
import jax.numpy as jnp
from jax import lax
from jax.experimental import pallas as pl
from jax.experimental.pallas import tpu as pltpu
from jax.sharding import PartitionSpec as P

MESH = pl.DeviceIdType.MESH
F32 = jnp.float32
BF16 = jnp.bfloat16
CHUNKS = 4
PART = 128
EXTRA = 2 * PART


def parts(chunk):
    return 1 if chunk < 1 else 2
CW, CCW = 0, 1


def hops(chunk, way):
    return 4 if chunk % 2 == way else 3


def expert_kernel(
    tokens_ref, ids_ref, logits_ref, placement_ref, split_ref, wh_hbm, ws_hbm, dh_hbm, ds_hbm, out_ref,
    tok, tab, tab_sibling, tok_extra, send, send_extra, mine, mine_extra, feat, pair_feat, hid, acc_h, acc_s, part, pair_part,
    out, back, combine, mix, mix_sibling, wh_raw, wide, wh_ref, wh_extra, ws_ref, dh_ref, ds_ref, dspare,
    ring_send, ring_recv, pair_send, pair_recv, hid_send, hid_recv, part_send, part_recv,
    load_sem, swap_send, swap_recv, go_send, go_recv, own_sem, back_send, back_recv,
    peer_send, peer_recv, extra_send, extra_recv,
):
    n_dp, n_z, n_x = 8, 8, 4
    n_chips = n_z * n_x
    ep = lax.axis_index("ep")
    me = lax.axis_index("dp")
    core = lax.rem(ep, 2)
    chip = ep // 2
    at_x = lax.rem(chip, n_x)
    at_z = chip // n_x
    sibling = {"ep": ep + 1 - 2 * core, "dp": me}
    ring = (
        {"ep": ep, "dp": lax.rem(me + 1, n_dp)},
        {"ep": ep, "dp": lax.rem(me + n_dp - 1, n_dp)},
    )

    def chip_at(dx, dz):
        return lax.rem(at_z + dz, n_z) * n_x + lax.rem(at_x + dx, n_x)

    loads = [
        pltpu.make_async_copy(src, dst, load_sem.at[i])
        for i, (src, dst) in enumerate(
            ((wh_hbm, wh_raw), (ws_hbm, ws_ref), (dh_hbm, dh_ref), (ds_hbm, ds_ref))
        )
    ]
    for load in loads:
        load.start()

    barrier = pltpu.get_barrier_semaphore()
    pl.semaphore_signal(barrier, inc=1, device_id=sibling, device_id_type=MESH)

    def dp_peer(step):
        return {"ep": ep, "dp": lax.rem(me + step, n_dp)}

    @pl.loop(1, n_dp)
    def _(step):
        pl.semaphore_signal(barrier, inc=1, device_id=dp_peer(step), device_id_type=MESH)

    @pl.loop(1, n_chips)
    def _(step):
        other = lax.rem(chip + step, n_chips)
        pl.semaphore_signal(
            barrier, inc=1, device_id={"ep": other * 2 + core, "dp": me}, device_id_type=MESH
        )

    group = tokens_ref.shape[0]
    width = tokens_ref.shape[1]
    half = width // 2
    block = 16

    def home_width(chunk):
        return width - parts(chunk) * PART

    def ring_width(chunk):
        return half + home_width(chunk)

    def extra_width(chunk):
        return parts(chunk) * n_dp * PART

    rows = n_z * block
    units = dh_hbm.shape[0] // n_dp
    top_k = ids_ref.shape[0]
    experts_ = 2 * n_chips
    lanes = 2 * group
    slot_rows = n_chips * block

    score = 1.0 / (1.0 + jnp.exp(-logits_ref[...]))
    weight = 2.5 * score / jnp.sum(score, axis=0, keepdims=True)
    high = weight.astype(BF16).astype(F32)
    stack = jnp.concatenate([ids_ref[...].astype(F32), high, weight - high], axis=0).astype(BF16)
    place = lax.broadcasted_iota(jnp.int32, (group, lanes), 1) - core * group
    spot = (place == lax.broadcasted_iota(jnp.int32, (group, lanes), 0)).astype(F32).astype(BF16)
    stack = jnp.dot(stack, spot, preferred_element_type=F32)
    row = lax.broadcasted_iota(jnp.int32, (experts_, lanes), 0)
    lane = lax.broadcasted_iota(jnp.int32, (experts_, lanes), 1)
    expert = row % n_chips * 2 + row // n_chips
    here = lane // group == core
    hit = jnp.zeros((experts_, lanes), F32)
    high = jnp.zeros((experts_, lanes), F32)
    rest = jnp.zeros((experts_, lanes), F32)
    for k in range(top_k):
        same = (stack[k : k + 1, :] == expert.astype(F32)) & here
        hit += jnp.where(same, 1.0, 0.0)
        high += jnp.where(same, stack[top_k + k : top_k + k + 1, :], 0.0)
        rest += jnp.where(same, stack[2 * top_k + k : 2 * top_k + k + 1, :], 0.0)
    earlier = lax.broadcasted_iota(jnp.int32, (lanes, lanes), 0) < lax.broadcasted_iota(jnp.int32, (lanes, lanes), 1)
    rank = jnp.dot(hit.astype(BF16), earlier.astype(F32).astype(BF16), preferred_element_type=F32)
    hot = jnp.zeros((experts_, lanes), F32)
    split = jnp.zeros((experts_, lanes), F32)
    spares = placement_ref.shape[0]
    spare_row = lax.broadcasted_iota(jnp.int32, (spares, experts_), 0)
    placed = jnp.zeros((spares, experts_), jnp.int32)
    for r in range(spares):
        chosen = expert == placement_ref[r]
        hot += jnp.where(chosen, 1.0, 0.0)
        split += jnp.where(chosen, split_ref[r].astype(F32), 0.0)
        placed = jnp.where(spare_row == r, placement_ref[r], placed)
    column = lax.broadcasted_iota(jnp.int32, (spares, experts_), 1)
    match = (placed == column % n_chips * 2 + column // n_chips).astype(F32).astype(BF16)
    moved = (hot > 0.0) & (rank >= split)
    capacity = 8.0
    home_code = jnp.where((hit > 0.0) & ~moved & (rank < capacity), rank + 1.0, 0.0)
    over = rank - split
    spare_code = jnp.where((hit > 0.0) & moved & (over < capacity), over + 1.0, 0.0)
    for i, (table, given) in enumerate(((home_code, spare_code), (high, high), (rest, rest))):
        base = i * (experts_ + spares)
        tab[pl.ds(base, experts_), :] = table
        tab[pl.ds(base + experts_, spares), :] = jnp.dot(match, given.astype(BF16), preferred_element_type=F32)

    loads[0].wait()

    @pl.loop(0, n_dp)
    def _(at):
        wide[...] = wh_raw[pl.ds(pl.multiple_of(at * 2 * width, 2 * width), 2 * width), :].astype(F32)
        for j in range(2):
            plain = wide[pl.ds(j, width, stride=2), :].astype(BF16)
            wh_ref[pl.ds(pl.multiple_of(at * width, width), width), j * units : (j + 1) * units] = plain
            for part_at in range(2):
                end = width - part_at * PART
                wh_extra[part_at, pl.ds(pl.multiple_of(at * PART, PART), PART), j * units : (j + 1) * units] = (
                    plain[end - PART : end]
                )

    pl.semaphore_wait(barrier, n_chips + n_dp - 1)

    own_tokens = pl.ds(pl.multiple_of(core * group, group), group)
    swaps = [
        pltpu.make_async_remote_copy(
            src_ref=src, dst_ref=dst, send_sem=swap_send.at[i], recv_sem=swap_recv.at[i],
            device_id=sibling, device_id_type=MESH,
        )
        for i, (src, dst) in enumerate(((tokens_ref, tok.at[own_tokens]), (tab, tab_sibling)))
    ]
    for swap in swaps:
        swap.start()

    def peer_copy(step):
        return pltpu.make_async_remote_copy(
            src_ref=tokens_ref.at[:, pl.ds(width - EXTRA, EXTRA)],
            dst_ref=tok_extra.at[me, own_tokens],
            send_sem=peer_send, recv_sem=peer_recv,
            device_id=dp_peer(step), device_id_type=MESH,
        )

    @pl.loop(1, n_dp)
    def _(step):
        peer_copy(step).start()

    tok[own_tokens, :] = tokens_ref[...]
    tok_extra[me, own_tokens, :] = tokens_ref[:, width - EXTRA :]
    for swap in swaps:
        swap.wait_recv()

    row = lax.broadcasted_iota(jnp.int32, (slot_rows, lanes), 0)
    lane = lax.broadcasted_iota(jnp.int32, (slot_rows, lanes), 1)
    in_group = row % block // 8 == lane // group
    wanted = (row % 8 + 1).astype(F32)

    def spread(i, spare):
        base = i * (experts_ + spares) + (experts_ if spare else core * n_chips)
        window = pl.ds(pl.multiple_of(base, n_chips), n_chips)
        table = tab[window, :] + tab_sibling[window, :]
        return jnp.broadcast_to(table[:, None, :], (n_chips, block, lanes)).reshape(slot_rows, lanes)

    def picked(spare):
        return (spread(0, spare) == wanted) & in_group

    home_pick = picked(False).astype(F32).astype(BF16)
    widest = home_width(0)
    send[:, half:] = jnp.dot(home_pick, tok[:, :widest], preferred_element_type=F32).astype(BF16)
    send[:, :half] = jnp.dot(
        picked(True).astype(F32).astype(BF16),
        tok[:, pl.ds(pl.multiple_of(core * half, half), half)],
        preferred_element_type=F32,
    ).astype(BF16)

    def go_copy(dx, dz):
        other = chip_at(dx, dz)
        return pltpu.make_async_remote_copy(
            src_ref=send.at[pl.ds(other * block, block), pl.ds(0, ring_width(dx))],
            dst_ref=mine.at[pl.ds((dx * n_z + at_z) * block, block), pl.ds(0, ring_width(dx))],
            send_sem=go_send.at[dx], recv_sem=go_recv.at[dx],
            device_id={"ep": other * 2 + core, "dp": me}, device_id_type=MESH,
        )

    own_go = pltpu.make_async_copy(
        send.at[pl.ds(chip * block, block), pl.ds(0, ring_width(0))],
        mine.at[pl.ds(at_z * block, block), pl.ds(0, ring_width(0))],
        own_sem.at[0],
    )
    own_go.start()
    for dx in range(n_x):
        @pl.loop(0 if dx else 1, n_z)
        def _(dz):
            go_copy(dx, dz).start()

    peers_in = tok_extra.at[pl.ds(0, n_dp - 1), pl.ds(0, group)]
    extra_swap = pltpu.make_async_remote_copy(
        src_ref=tok_extra.at[:, own_tokens], dst_ref=tok_extra.at[:, own_tokens],
        send_sem=swap_send.at[3], recv_sem=swap_recv.at[3], device_id=sibling, device_id_type=MESH,
    )

    def swap_extras():
        pltpu.make_async_copy(peers_in, peers_in, peer_recv).wait()
        extra_swap.start()

    def extra_copy(dx, dz):
        other = chip_at(dx, dz)
        return pltpu.make_async_remote_copy(
            src_ref=send_extra.at[pl.ds(other * block, block), pl.ds(0, extra_width(dx))],
            dst_ref=mine_extra.at[pl.ds((dx * n_z + at_z) * block, block), pl.ds(0, extra_width(dx))],
            send_sem=extra_send.at[dx], recv_sem=extra_recv.at[dx],
            device_id={"ep": other * 2 + core, "dp": me}, device_id_type=MESH,
        )

    own_extra = pltpu.make_async_copy(
        send_extra.at[pl.ds(chip * block, block), pl.ds(0, extra_width(0))],
        mine_extra.at[pl.ds(at_z * block, block), pl.ds(0, extra_width(0))],
        own_sem.at[2],
    )

    def send_extras():
        extra_swap.wait_recv()
        for at in range(n_dp):
            both = jnp.dot(home_pick, tok_extra[at], preferred_element_type=F32).astype(BF16)
            send_extra[:, at * PART : (at + 1) * PART] = both[:, PART:]
            send_extra[:, (n_dp + at) * PART : (n_dp + at + 1) * PART] = both[:, :PART]
        own_extra.start()
        for dx in range(n_x):
            @pl.loop(0 if dx else 1, n_z)
            def _(dz):
                extra_copy(dx, dz).start()

    def source(way, hop):
        return lax.rem(me + (n_dp - hop if way == CW else hop), n_dp)

    def feat_copy(chunk, way, hop):
        src = source(way, hop - 1)
        window = pl.ds(chunk * rows, rows)
        cols = pl.ds(0, ring_width(chunk))
        return pltpu.make_async_remote_copy(
            src_ref=mine.at[window, cols] if hop == 1 else feat.at[src, window, cols],
            dst_ref=feat.at[src, window, cols],
            send_sem=ring_send.at[chunk, way, hop - 1],
            recv_sem=ring_recv.at[chunk, way, hop - 1],
            device_id=ring[way], device_id_type=MESH,
        )

    def pair_copy(chunk, way, hop):
        src = source(way, hop)
        window = pl.ds(chunk * rows, rows)
        here = mine.at[window, pl.ds(0, half)] if hop == 0 else feat.at[src, window, pl.ds(0, half)]
        return pltpu.make_async_remote_copy(
            src_ref=here,
            dst_ref=pair_feat.at[src, window],
            send_sem=pair_send.at[chunk, way, hop],
            recv_sem=pair_recv.at[chunk, way, hop],
            device_id=sibling, device_id_type=MESH,
        )

    hid_rows = rows + rows // 2

    def hid_copy(chunk, way, hop):
        src = source(way, hop - 1)
        window = pl.ds(chunk * hid_rows, hid_rows)
        return pltpu.make_async_remote_copy(
            src_ref=hid.at[src, window],
            dst_ref=hid.at[src, window],
            send_sem=hid_send.at[chunk, way, hop - 1],
            recv_sem=hid_recv.at[chunk, way, hop - 1],
            device_id=ring[way], device_id_type=MESH,
        )

    columns = ds_ref.shape[1]
    out_half = columns // 2

    def part_copy(chunk):
        window = pl.ds(chunk * rows, rows)
        return pltpu.make_async_remote_copy(
            src_ref=part.at[window, pl.ds((1 - core) * out_half, out_half)],
            dst_ref=pair_part.at[window],
            send_sem=part_send.at[chunk],
            recv_sem=part_recv.at[chunk],
            device_id=sibling, device_id_type=MESH,
        )

    def back_copy(dx, dz):
        z = lax.rem(at_z + dz, n_z)
        other = chip_at(n_x - dx, dz)
        return pltpu.make_async_remote_copy(
            src_ref=out.at[pl.ds((dx * n_z + z) * block, block)],
            dst_ref=back.at[pl.ds(chip * block, block)],
            send_sem=back_send, recv_sem=back_recv,
            device_id={"ep": other * 2 + core, "dp": me}, device_id_type=MESH,
        )

    turned_dims = (((1,), (1,)), ((), ()))

    def spare_term(x, at, side):
        cols = pl.ds(pl.multiple_of(at * width + side * half, half), half)
        return lax.dot_general(x, ws_ref[:, cols], turned_dims, preferred_element_type=F32)

    def project(x, at):
        depth = x.shape[1] - half
        w = wh_ref[pl.ds(pl.multiple_of(at * width, width), depth), :]
        home = jnp.dot(x[:, half:], w, preferred_element_type=F32)
        return home, spare_term(x[:, :half], at, core)

    def begin(chunk):
        window = pl.ds(chunk * rows, rows)
        arrived = mine.at[pl.ds(chunk * rows, rows if chunk else rows - block), pl.ds(0, ring_width(chunk))]
        pltpu.make_async_copy(arrived, arrived, go_recv.at[chunk]).wait()
        if chunk == 0:
            own_go.wait()
        for way in (CW, CCW):
            feat_copy(chunk, way, 1).start()
        pair_copy(chunk, CW, 0).start()
        if chunk == 0:
            loads[1].wait()
        acc_h[window, :], acc_s[window, :] = project(mine[window, : ring_width(chunk)], me)

    def add_pair(chunk, way, hop):
        window = pl.ds(chunk * rows, rows)
        src = source(way, hop)
        pair_copy(chunk, way, hop).wait_recv()
        acc_s[window, :] += spare_term(pair_feat[src, window, :], src, 1 - core)

    def arrive(chunk, hop):
        window = pl.ds(chunk * rows, rows)
        ways = [way for way in (CW, CCW) if hop <= hops(chunk, way)]
        for way in ways:
            feat_copy(chunk, way, hop).wait_recv()
            if hop < hops(chunk, way):
                feat_copy(chunk, way, hop + 1).start()
            pair_copy(chunk, way, hop).start()
        for way in ways:
            src = source(way, hop)
            home, spare = project(feat[src, window, : ring_width(chunk)], src)
            acc_h[window, :] += home
            acc_s[window, :] += spare
        if hop == 1:
            add_pair(chunk, CW, 0)
        else:
            for way in (CW, CCW):
                add_pair(chunk, way, hop - 1)

    def first_half(chunk):
        window = pl.ds(chunk * rows, rows)
        for way in (CW, CCW):
            if hops(chunk, way) == 4:
                add_pair(chunk, way, 4)
        came = mine_extra.at[pl.ds(chunk * rows, rows if chunk else rows - block), pl.ds(0, extra_width(chunk))]
        pltpu.make_async_copy(came, came, extra_recv.at[chunk]).wait()
        if chunk == 0:
            own_extra.wait()
        for part_at in range(parts(chunk)):
            x = mine_extra[window, part_at * n_dp * PART : (part_at + 1) * n_dp * PART]
            acc_h[window, :] += jnp.dot(x, wh_extra[part_at], preferred_element_type=F32)
        gate = acc_h[window, :units]
        base = chunk * hid_rows
        hid[me, pl.ds(base, rows), :] = (gate / (1.0 + jnp.exp(-gate)) * acc_h[window, units:]).astype(BF16)
        plain = acc_s[window, :]
        turned = pltpu.roll(plain, units // 2, 1)
        low = lax.broadcasted_iota(jnp.int32, plain.shape, 1) < units // 2
        gate = jnp.where(low, plain, turned)
        both = gate / (1.0 + jnp.exp(-gate)) * jnp.where(low, turned, plain)
        top = rows // 2
        packed = jnp.where(low[:top], both[:top], both[top:])
        hid[me, pl.ds(base + rows, top), :] = packed.astype(BF16)
        for way in (CW, CCW):
            hid_copy(chunk, way, 1).start()

    def hid_arrive(chunk, hop):
        for way in (CW, CCW):
            if hop <= hops(chunk, way):
                hid_copy(chunk, way, hop).wait_recv()
                if hop < hops(chunk, way):
                    hid_copy(chunk, way, hop + 1).start()

    def second_half(chunk):
        window = pl.ds(chunk * rows, rows)
        base = chunk * hid_rows
        top = rows // 2
        packed = jnp.concatenate([hid[at, pl.ds(base + rows, top), :] for at in range(n_dp)], axis=1)
        low = lax.broadcasted_iota(jnp.int32, packed.shape, 1) % units < units // 2
        none = jnp.zeros_like(packed)
        both = jnp.concatenate([jnp.where(low, packed, none), jnp.where(low, none, packed)], axis=0)
        part[window, :] = jnp.dot(both, dspare[...], preferred_element_type=F32)
        part_copy(chunk).start()
        whole = jnp.concatenate([hid[at, pl.ds(base, rows), :] for at in range(n_dp)], axis=1)
        out[window, :columns] = jnp.dot(whole, dh_ref[...], preferred_element_type=F32).astype(BF16)

    own_back = pltpu.make_async_copy(
        out.at[pl.ds(at_z * block, block)], back.at[pl.ds(chip * block, block)], own_sem.at[1]
    )

    def finish(chunk):
        window = pl.ds(chunk * rows, rows)
        part_copy(chunk).wait_recv()
        own = part[window, pl.ds(pl.multiple_of(core * out_half, out_half), out_half)]
        out[window, columns:] = (own + pair_part[window, :]).astype(BF16)
        if chunk == 0:
            own_back.start()

        @pl.loop(0 if chunk else 1, n_z)
        def _(dz):
            back_copy(chunk, dz).start()

    def prepare():
        for i, spare in enumerate((False, True)):
            for j in range(2):
                combine[2 * i + j] = jnp.where(picked(spare), spread(1 + j, spare), 0.0).T.astype(BF16)
        loads[2].wait()
        loads[3].wait()
        for at in range(n_dp):
            w = ds_ref[pl.ds(at * units // 2, units // 2), :]
            dspare[pl.ds(at * units, units // 2), :] = w
            dspare[pl.ds(at * units + units // 2, units // 2), :] = w

    events = []
    for chunk in range(CHUNKS):
        for hop in range(5):
            events.append((chunk + hop, 0, -chunk, "feat", chunk, hop))
        events.append((chunk + 4, 1, -chunk, "first", chunk, 0))
        for hop in range(1, 5):
            events.append((chunk + 4 + hop, 2, -chunk, "hid", chunk, hop))
        events.append((chunk + 8, 3, -chunk, "second", chunk, 0))
        events.append((chunk + 9, 4, -chunk, "finish", chunk, 0))
    events.append((0, 9, 0, "prepare", 0, 0))
    events.append((0, 0, 9, "peers", 0, 0))
    events.append((0, 0, 10, "extra", 0, 0))
    for _, _, _, kind, chunk, hop in sorted(events):
        if kind == "feat":
            arrive(chunk, hop) if hop else begin(chunk)
        elif kind == "first":
            first_half(chunk)
        elif kind == "hid":
            hid_arrive(chunk, hop)
        elif kind == "second":
            second_half(chunk)
        elif kind == "finish":
            finish(chunk)
        elif kind == "extra":
            send_extras()
        elif kind == "peers":
            swap_extras()
        else:
            prepare()

    landed = back.at[pl.ds(0, (n_chips - 1) * block)]
    pltpu.make_async_copy(landed, landed, back_recv).wait()
    own_back.wait()

    def weigh(i, who, table):
        return jnp.dot(combine[2 * i, who, :], table, preferred_element_type=F32) + jnp.dot(
            combine[2 * i + 1, who, :], table, preferred_element_type=F32
        )

    side = pl.ds(pl.multiple_of(core * out_half, out_half), out_half)

    def mix_group(which):
        who = pl.ds(pl.multiple_of(which * group, group), group)
        mix[who, :] = weigh(0, who, back[:, :columns])
        mix[who, side] += weigh(1, who, back[:, columns:])

    mix_group(1 - core)
    mix_swap = pltpu.make_async_remote_copy(
        src_ref=mix.at[pl.ds((1 - core) * group, group)], dst_ref=mix_sibling,
        send_sem=swap_send.at[2], recv_sem=swap_recv.at[2],
        device_id=sibling, device_id_type=MESH,
    )
    mix_swap.start()
    mix_group(core)
    mix_swap.wait_recv()
    out_ref[...] = (mix[pl.ds(pl.multiple_of(core * group, group), group), :] + mix_sibling[...]).astype(out_ref.dtype)

    mix_swap.wait_send()
    extra_swap.wait_send()
    pltpu.make_async_copy(peers_in, peers_in, peer_send).wait()
    for chunk in range(CHUNKS):
        count = rows if chunk else rows - block
        gone = send_extra.at[pl.ds(0, count), pl.ds(0, extra_width(chunk))]
        pltpu.make_async_copy(gone, gone, extra_send.at[chunk]).wait()
        gone = send.at[pl.ds(0, count), pl.ds(0, ring_width(chunk))]
        pltpu.make_async_copy(gone, gone, go_send.at[chunk]).wait()
    for swap in swaps:
        swap.wait_send()
    gone = out.at[pl.ds(0, (n_chips - 1) * block)]
    pltpu.make_async_copy(gone, gone, back_send).wait()
    for chunk in range(CHUNKS):
        for way in (CW, CCW):
            for hop in range(1, hops(chunk, way) + 1):
                feat_copy(chunk, way, hop).wait_send()
                hid_copy(chunk, way, hop).wait_send()
                pair_copy(chunk, way, hop).wait_send()
        pair_copy(chunk, CW, 0).wait_send()
        part_copy(chunk).wait_send()


def experts(tokens, ids, logits, placement, split_rows, wh, ws, dh, ds):
    group, width = tokens.shape
    n_dp = 8
    half = width // 2
    lean = width - PART
    units = wh.shape[1]
    total = 512
    columns = ds.shape[1]
    lanes = 2 * group
    table_rows = 3 * (64 + placement.shape[0])
    dma = pltpu.SemaphoreType.DMA
    ring_sems = dma((CHUNKS, 2, 4))
    pair_sems = dma((CHUNKS, 2, 5))
    part_sems = dma((CHUNKS,))
    in_vmem = pl.BlockSpec(memory_space=pltpu.VMEM)
    in_smem = pl.BlockSpec(memory_space=pltpu.SMEM)
    in_hbm = pl.BlockSpec(memory_space=pl.ANY)
    return pl.pallas_call(
        expert_kernel,
        out_shape=jax.ShapeDtypeStruct((group, columns), F32),
        in_specs=[in_vmem] * 3 + [in_smem] * 2 + [in_hbm] * 4,
        out_specs=in_vmem,
        scratch_shapes=[
            pltpu.VMEM((lanes, width), BF16),
            pltpu.VMEM((table_rows, lanes), F32),
            pltpu.VMEM((table_rows, lanes), F32),
            pltpu.VMEM((n_dp, lanes, EXTRA), BF16),
            pltpu.VMEM((total, lean + half), BF16),
            pltpu.VMEM((total, n_dp * EXTRA), BF16),
            pltpu.VMEM((total, lean + half), BF16),
            pltpu.VMEM((total, n_dp * EXTRA), BF16),
            pltpu.VMEM((n_dp, total, lean + half), BF16),
            pltpu.VMEM((n_dp, total, half), BF16),
            pltpu.VMEM((n_dp, total + total // 2, units), BF16),
            pltpu.VMEM((total, 2 * units), F32),
            pltpu.VMEM((total, units), F32),
            pltpu.VMEM((total, columns), F32),
            pltpu.VMEM((total, columns // 2), F32),
            pltpu.VMEM((total, columns + columns // 2), BF16),
            pltpu.VMEM((total, columns + columns // 2), BF16),
            pltpu.VMEM((4, lanes, total), BF16),
            pltpu.VMEM((lanes, columns), F32),
            pltpu.VMEM((group, columns), F32),
            pltpu.VMEM(wh.shape, BF16),
            pltpu.VMEM((2 * width, units), F32),
            pltpu.VMEM((n_dp * width, 2 * units), BF16),
            pltpu.VMEM((2, n_dp * PART, 2 * units), BF16),
            pltpu.VMEM(ws.shape, BF16),
            pltpu.VMEM(dh.shape, BF16),
            pltpu.VMEM(ds.shape, BF16),
            pltpu.VMEM((n_dp * units, columns), BF16),
            ring_sems, ring_sems, pair_sems, pair_sems, ring_sems, ring_sems, part_sems, part_sems,
            dma((4,)), dma((4,)), dma((4,)), dma((4,)), dma((4,)), dma((3,)), dma, dma,
            dma, dma, dma((4,)), dma((4,)),
        ],
        compiler_params=pltpu.CompilerParams(
            collective_id=0, has_side_effects=True, vmem_limit_bytes=56 * 1024 * 1024
        ),
    )(tokens, ids, logits, placement, split_rows, wh, ws, dh, ds)


def per_device(
    tokens, expert_ids, gate_logits, placement, split_rows,
    gate_up_weight, down_weight, spare_gate_up, spare_down,
):
    wh = gate_up_weight.reshape(-1, gate_up_weight.shape[3])
    ws = jnp.transpose(spare_gate_up[0], (1, 2, 0)).reshape(-1, spare_gate_up.shape[1])
    return experts(
        tokens, expert_ids.T, gate_logits.T, placement, split_rows, wh, ws, down_weight[0], spare_down[0]
    ).astype(BF16)


def solution(mesh):
    return jax.shard_map(
        per_device,
        mesh=mesh,
        in_specs=(
            P("ep", "dp"),
            P("ep", None),
            P("ep", None),
            P(),
            P(),
            P("ep", None, None, "dp"),
            P("ep", None, "dp"),
            P("ep", None, None, "dp"),
            P("ep", None, "dp"),
        ),
        out_specs=P("ep", "dp"),
        check_vma=False,
    )
```
